512 devices in a mesh: tensor: 32 (over y, x, core), replica: 16 (over z).
Axes of the slice: x: 4, y: 4, z: 16, core: 2. Of those that a mesh axis runs over, the one named last changes fastest.
Arguments:
- hidden_in: bfloat16 [12288, 4096], P(('replica', 'tensor')), parts along dimension 0, may hold values from -6 to 6
- query_weight: bfloat16 [4096, 8192], P('tensor'), as said below
- key_weight: bfloat16 [4096, 1024], P('tensor'), as said below
- value_projection_weight: bfloat16 [4096, 1024], P('tensor'), may hold values from -0.09375 to 0.09375
- output_weight: bfloat16 [8192, 4096], P('tensor'), may hold values from -0.5 to 0.5
- head_order: int32 [64], replicated, may hold values from 0 to 63, each once
- positions: int32 [12288], P('replica'), parts along dimension 0, may hold values from 0 to 383, as said below
Outputs:
- attended: bfloat16 [12288, 4096], P(('replica', 'tensor')), parts along dimension 0
The draws below stay inside these ranges and needn't reach their ends.
There are 16 independent parts, one for each index of `replica`. The reference program is written for one: setup_inputs(seed, part) draws one part's arguments, and reference() takes and returns one part's arrays. A program takes and returns all parts, laid end to end along the dimension named above; an argument that names none is the same for every part. Nothing has to cross between parts.
Inputs may be any that keep to these rules, and one draw needn't show every extreme that they name: `head_order`: each of 0 to 63 appears once. `positions`: each token's position counts up from 0 at the start of its document; token 0 starts a document. `query_weight`: finite projection weights. `key_weight`: finite projection weights.
All inputs are finite; a program needn't handle non-finite values.
Results may differ from the reference program's by a relative error of at most 0.02.
Values may be sent and summed in bfloat16 or wider, within the bound.
A program may use at most 64 MiB of HBM per device.

```python
import math
import jax
import jax.numpy as jnp
from jax import lax

FEATURE_SLICE = 4096
HEAD_SIZE = 128
HQ_W = 64
KEY_VALUE_HEADS = 8
PROMPT_TOKENS = 768
GROUP = 8
HEADS_DEV = 2
N_TENSOR = 32


def draw_query_weight(key, part):
    key = jax.random.fold_in(key, 11)
    random_noise_term = jax.random.normal(key, (FEATURE_SLICE, HQ_W, HEAD_SIZE), jnp.float32) / math.sqrt(FEATURE_SLICE)
    weight_tensors = random_noise_term
    return weight_tensors.reshape(FEATURE_SLICE, HQ_W * HEAD_SIZE).astype(jnp.bfloat16)


def draw_key_weight(key, part):
    key = jax.random.fold_in(key, 13)
    random_noise_term = jax.random.normal(key, (FEATURE_SLICE, KEY_VALUE_HEADS, HEAD_SIZE), jnp.float32) / math.sqrt(FEATURE_SLICE)
    weight_tensors = random_noise_term
    return weight_tensors.reshape(FEATURE_SLICE, KEY_VALUE_HEADS * HEAD_SIZE).astype(jnp.bfloat16)


def draw_positions(key, part):
    key = jax.random.fold_in(key, 17)
    start_key = jax.random.fold_in(key, 1)
    forced_key = jax.random.fold_in(key, 2)
    index_row = jnp.arange(PROMPT_TOKENS, dtype=jnp.int32)
    half_point = PROMPT_TOKENS // 2
    starts = jax.random.randint(start_key, (PROMPT_TOKENS,), 0, 6) == 0
    starts = jnp.logical_and(starts, index_row > half_point)
    forced = jax.random.randint(forced_key, (), half_point + 1, PROMPT_TOKENS)
    starts = jnp.logical_or(starts, index_row == forced)
    starts = jnp.logical_or(starts, index_row == 0)
    starts = jnp.logical_or(starts, index_row == half_point)
    marked = jnp.where(starts, index_row, 0)
    latest = lax.cummax(marked, axis=0)
    return (index_row - latest).astype(jnp.int32)


def block_levels(rng, extent, split, smallest, largest):
    loudness = 1.0
    for axis_at, blocks in split:
        draws = jax.random.uniform(jax.random.fold_in(jax.random.fold_in(rng, 6), axis_at), (blocks,), jnp.float32, smallest / len(split), largest / len(split))
        loudness = loudness * jnp.repeat(jnp.exp(draws), extent[axis_at] // blocks).reshape((-1,) + (1,) * (len(extent) - 1 - axis_at))
    return loudness


def noise(key, extent, deviation, limit, cuts=(), kind=jnp.bfloat16):
    result = deviation * jax.random.normal(key, extent, jnp.float32)
    if cuts:
        result = result * block_levels(key, extent, cuts, -0.22, 0.18)
    return jnp.clip(result, -limit, limit).astype(kind)


def setup_inputs(seed: int = 0, part: int = 0) -> dict:
    seeds = jax.random.split(jax.random.key(seed), 8)
    part_splits = jax.random.split(jax.random.fold_in(seeds[7], part), 8)
    return {
        "hidden_in": noise(part_splits[0], (PROMPT_TOKENS, FEATURE_SLICE), 1.0, 6.0, ((0, 32),)),
        "query_weight": draw_query_weight(jax.random.fold_in(seeds[7], 71), part),
        "key_weight": draw_key_weight(jax.random.fold_in(seeds[7], 71), part),
        "value_projection_weight": noise(seeds[3], (FEATURE_SLICE, KEY_VALUE_HEADS * HEAD_SIZE), FEATURE_SLICE ** -0.5, 0.09375, ((0, 32),)),
        "output_weight": noise(seeds[4], (HQ_W * HEAD_SIZE, FEATURE_SLICE), HEAD_SIZE ** -0.5, 0.5, ((0, 32),)),
        "head_order": jax.random.permutation(seeds[5], HQ_W).astype(jnp.int32),
        "positions": draw_positions(jax.random.fold_in(jax.random.fold_in(seeds[7], part), 71), part),
    }


rope_base = 1000000.0


def rotate_pairs(values_in, positions):
    half_width = HEAD_SIZE // 2
    frequency = rope_base ** (-2.0 * jnp.arange(half_width, dtype=jnp.float32) / HEAD_SIZE)
    angles = positions.astype(jnp.float32)[:, None] * frequency[None, :]
    cosine = jnp.cos(angles)[:, None, :]
    sine_part = jnp.sin(angles)[:, None, :]
    front_half = values_in[..., :half_width]
    back_half = values_in[..., half_width:]
    return jnp.concatenate([front_half * cosine - back_half * sine_part, back_half * cosine + front_half * sine_part], axis=-1)


def reference(hidden_in, query_weight, key_weight, value_projection_weight, output_weight, head_order, positions):
    inverse = jnp.argsort(head_order).astype(jnp.int32)
    query_cols = jnp.take(query_weight.reshape(FEATURE_SLICE, HQ_W, HEAD_SIZE), inverse, axis=1).reshape(FEATURE_SLICE, HQ_W * HEAD_SIZE)
    query_raw = jnp.dot(hidden_in, query_cols, preferred_element_type=jnp.float32).reshape(PROMPT_TOKENS, HQ_W, HEAD_SIZE)
    queries = rotate_pairs(query_raw, positions).astype(jnp.bfloat16)
    key_unprojected = jnp.dot(hidden_in, key_weight, preferred_element_type=jnp.float32).astype(jnp.bfloat16)
    key_unprojected = key_unprojected.reshape(PROMPT_TOKENS, KEY_VALUE_HEADS, HEAD_SIZE)
    keys = rotate_pairs(key_unprojected.astype(jnp.float32), positions).astype(jnp.bfloat16)
    value_token_rows = jnp.dot(hidden_in, value_projection_weight, preferred_element_type=jnp.float32).astype(jnp.bfloat16)
    value_token_rows = value_token_rows.reshape(PROMPT_TOKENS, KEY_VALUE_HEADS, HEAD_SIZE)
    causal = jnp.arange(PROMPT_TOKENS)[:, None] >= jnp.arange(PROMPT_TOKENS)[None, :]

    def one_head(head_index):
        kv_index = head_index // GROUP
        query_head = jnp.take(queries, head_index, axis=1)
        key_head = jnp.take(keys, kv_index, axis=1)
        value_head = jnp.take(value_token_rows, kv_index, axis=1)
        scores = jnp.dot(query_head, key_head.T, preferred_element_type=jnp.float32) * (HEAD_SIZE ** -0.5)
        scores = jnp.where(causal, scores, -jnp.inf)
        top = jnp.max(scores, axis=1, keepdims=True)
        expo = jnp.exp(scores - top)
        probs = (expo / jnp.sum(expo, axis=1, keepdims=True)).astype(jnp.bfloat16)
        return jnp.dot(probs, value_head, preferred_element_type=jnp.float32).astype(jnp.bfloat16)

    head_out = lax.map(one_head, jnp.arange(HQ_W, dtype=jnp.int32))
    head_blocks = head_out.reshape(N_TENSOR, HEADS_DEV, PROMPT_TOKENS, HEAD_SIZE)
    weight_blocks = output_weight.reshape(N_TENSOR, HEADS_DEV * HEAD_SIZE, FEATURE_SLICE)

    def add_block(total, pair):
        block_out, block_weight = pair
        flat = jnp.transpose(block_out, (1, 0, 2)).reshape(PROMPT_TOKENS, HEADS_DEV * HEAD_SIZE)
        partial_value = jnp.dot(flat, block_weight, preferred_element_type=jnp.float32)
        rounded = lax.optimization_barrier(partial_value.astype(jnp.bfloat16)).astype(jnp.float32)
        return total + rounded, None

    total, unused = lax.scan(add_block, jnp.zeros((PROMPT_TOKENS, FEATURE_SLICE), jnp.float32), (head_blocks, weight_blocks))
    return total.astype(jnp.bfloat16)
```

```python
import math

import jax
import jax.numpy as jnp
import numpy as np
from jax import lax
from jax.experimental import pallas as pl
from jax.experimental.pallas import tpu as pltpu
from jax.sharding import PartitionSpec as P

MESH = pl.DeviceIdType.MESH
F32, BF16 = jnp.float32, jnp.bfloat16

HEAD = 128
RING = 4
TOK = 48
ROWS = RING * TOK
SPAN = RING * ROWS
FEAT = 4096
DEPTH = FEAT // RING
KV_COLS = RING * HEAD
Q_COLS = RING * 2 * HEAD
HALF = FEAT // 2
ROPE_BASE = 1000000.0
EXP_SCALE = math.log2(math.e) / math.sqrt(HEAD)


def kernel(
    x_hbm, wq_hbm, wk_hbm, wv_hbm, wo_hbm, inv_ref, ang_ref,
    out_ref,
    xpair, xs, xall, wq, wkv, wsend, wall, wo2, cos_t, sin_t,
    ykv, ykv_in, yq, yq_in, kv, hbuf, obuf, o1_in, o1_sum, o2_in, fin_out, fin_in,
    loc_sem, d2d_s, d2d_r, w_s, w_r, x1_s, x2_s, x_r, ykv_s, ykv_r, yq_s, yq_r,
    h_s, h_r, o1_s, o1_r, o2_s, o2_r,
):
    t = lax.axis_index("tensor")
    y, x, c = t // 8, (t // 2) % 4, t % 2
    first = c == 0
    p, s = jnp.where(first, x, y), jnp.where(first, y, x)
    oc = 1 - c

    def wrap(v):
        return lax.rem(v + 8, RING)

    def device(pp, ss):
        return jnp.where(first, 8 * ss + 2 * pp, 8 * pp + 2 * ss + 1)

    def slot(pp, ss):
        yy, xx = jnp.where(first, ss, pp), jnp.where(first, pp, ss)
        return RING * wrap(xx - yy) + yy

    def remote(src, dst, ss, rs, dev):
        return pltpu.make_async_remote_copy(
            src_ref=src, dst_ref=dst, send_sem=ss, recv_sem=rs,
            device_id={"tensor": dev}, device_id_type=MESH,
        )

    partner = t + 1 - 2 * c

    own_x = pltpu.make_async_copy(x_hbm, xpair.at[c], loc_sem.at[0])
    own_q = pltpu.make_async_copy(wq, wq, loc_sem.at[1])
    own_k = pltpu.make_async_copy(wk_hbm, wkv.at[0], loc_sem.at[2])
    own_v = pltpu.make_async_copy(wv_hbm, wkv.at[1], loc_sem.at[3])
    own_o = pltpu.make_async_copy(
        wo_hbm.at[:, pl.ds(pl.multiple_of(c * HALF, HALF), HALF)], wo2.at[c], loc_sem.at[4]
    )

    def load_head(i, _):
        cols = pl.ds(pl.multiple_of(i * HEAD, HEAD), HEAD)
        pltpu.make_async_copy(wq_hbm.at[:, cols], wq.at[i], loc_sem.at[1]).start()
        return 0

    own_k.start()
    own_v.start()
    lax.fori_loop(0, 64, load_head, 0)
    own_x.start()
    own_o.start()

    barrier = pltpu.get_barrier_semaphore()

    def greet(dev):
        pl.semaphore_signal(barrier, inc=1, device_id={"tensor": dev}, device_id_type=MESH)

    greet(partner)
    for d in range(1, RING):
        ring = device(wrap(p + d), s)
        greet(ring)
        greet(ring + 1 - 2 * c)
        greet(device(p, wrap(s + d)))
    pl.semaphore_wait(barrier, 10)

    x_d2d = remote(x_hbm, xpair.at[c], d2d_s.at[0], d2d_r.at[0], partner)
    x_d2d.start()

    own_q.wait()
    own_k.wait()
    own_v.wait()
    w_copies = []
    for other in (0, 1):
        cc = jnp.where(other == 1, oc, c)
        cc_first = cc == 0
        pcc = jnp.where(cc_first, x, y)
        for d in (1, 2, 3, 0):
            pp = wrap(pcc + d)
            own = other == 0 and d == 0
            place = wall.at[2 * p + c] if own else wsend.at[RING * other + d]

            def fill(ss, _, place=place, cc=cc, cc_first=cc_first, pp=pp):
                tt = jnp.where(cc_first, 8 * ss + 2 * pp, 8 * pp + 2 * ss + 1)
                group = pl.multiple_of((tt // 4) * HEAD, HEAD)
                place[:, pl.ds(pl.multiple_of(ss * HEAD, HEAD), HEAD)] = wkv[
                    cc, :, pl.ds(group, HEAD)
                ]
                for i in range(2):
                    at = pl.multiple_of(KV_COLS + (2 * ss + i) * HEAD, HEAD)
                    place[:, pl.ds(at, HEAD)] = wq[inv_ref[2 * tt + i]]
                return 0

            lax.fori_loop(0, RING, fill, 0)
            if not own:
                dev = jnp.where(cc_first, 8 * y + 2 * pp, 8 * pp + 2 * x + 1)
                copy = remote(
                    place, wall.at[2 * pcc + c],
                    w_s.at[RING * other + d], w_r.at[2 * pcc + c], dev,
                )
                copy.start()
                w_copies.append(copy)

    own_x.wait()
    x_d2d.wait_send()
    remote(x_hbm, xpair.at[oc], d2d_s.at[0], d2d_r.at[0], partner).wait_recv()
    wo_d2d = remote(
        wo_hbm.at[:, pl.ds(pl.multiple_of(oc * HALF, HALF), HALF)], wo2.at[c],
        d2d_s.at[1], d2d_r.at[1], partner,
    )
    wo_d2d.start()
    mine = slot(p, s)
    x_copies = []
    for d in (1, 2, 3, 0):
        ss = wrap(s + d)
        for pp in range(RING):
            feat = pl.multiple_of(
                jnp.where(first, DEPTH * ss + 256 * pp, DEPTH * pp + 256 * ss), 256
            )
            rows = jnp.concatenate(
                [xpair[0, :, pl.ds(feat, 256)].astype(F32), xpair[1, :, pl.ds(feat, 256)].astype(F32)],
                axis=0,
            ).astype(BF16)
            if d == 0:
                xall[mine, :, 256 * pp : 256 * pp + 256] = rows
            else:
                xs[d, :, 256 * pp : 256 * pp + 256] = rows
        if d:
            copy = remote(xs.at[d], xall.at[mine], x1_s.at[d], x_r.at[mine], device(p, ss))
            copy.start()
            x_copies.append(copy)

    def arrived(m):
        remote(xall.at[m], xall.at[m], x1_s.at[0], x_r.at[m], partner).wait_recv()

    for d in range(RING):
        m = slot(p, wrap(s + d))
        if d:
            arrived(m)
        for e in (1, 2, 3):
            copy = remote(
                xall.at[m], xall.at[m], x2_s.at[RING * e + d], x_r.at[m], device(wrap(p + e), s)
            )
            copy.start()
            x_copies.append(copy)

    sign = jnp.where(lax.broadcasted_iota(jnp.int32, (TOK, HEAD), 1) < HEAD // 2, -1.0, 1.0)

    def table(n, _):
        at = pl.ds(pl.multiple_of(n * TOK, TOK), TOK)
        ang = ang_ref[at, :]
        cos_t[at, :] = jnp.cos(ang)
        sin_t[at, :] = jnp.sin(ang) * sign
        return 0

    lax.fori_loop(0, RING * RING, table, 0)

    own_o.wait()
    wo_d2d.wait()
    for e in range(RING):
        for cs in range(2):
            k = 2 * wrap(p + e) + (c if cs == 0 else oc)
            if e or cs:
                remote(wall.at[k], wall.at[k], w_s.at[0], w_r.at[k], partner).wait_recv()
    for e in (1, 2, 3):
        for ss in range(RING):
            arrived(slot(wrap(p + e), ss))

    def tokens(j):
        return xall[pl.ds(j * RING, RING)].reshape(ROWS, DEPTH)

    def partial_kv(j, _):
        r = jnp.dot(
            tokens(j), wall[:, :, :KV_COLS].reshape(DEPTH, KV_COLS), preferred_element_type=F32
        ).astype(BF16)
        at = pl.ds(pl.multiple_of(j * ROWS, ROWS), ROWS)
        for ss in range(RING):
            ykv[ss, at, :] = r[:, ss * HEAD : (ss + 1) * HEAD]
        return 0

    lax.fori_loop(0, RING, partial_kv, 0)
    y_copies = []
    for d in (2, 1, 3):
        ss = wrap(s + d)
        copy = remote(ykv.at[ss], ykv_in.at[s], ykv_s.at[d], ykv_r.at[s], device(p, ss))
        copy.start()
        y_copies.append(copy)
    for j in range(RING):
        r = jnp.dot(
            tokens(j), wall[:, :, KV_COLS:].reshape(DEPTH, Q_COLS), preferred_element_type=F32
        ).astype(BF16)
        for ss in range(RING):
            yq[j, ss] = r[:, ss * 2 * HEAD : (ss + 1) * 2 * HEAD]
        for d in (2, 1, 3):
            ss = wrap(s + d)
            copy = remote(
                yq.at[j, ss], yq_in.at[j, s], yq_s.at[j, d], yq_r.at[j, s], device(p, ss)
            )
            copy.start()
            y_copies.append(copy)

    def rotate(v, at):
        return v * cos_t[at, :] + pltpu.roll(v, HEAD // 2, 1) * sin_t[at, :]

    def place_of(j, b):
        return RING * b + (b + j) % RING

    for d in (1, 2, 3):
        ss = wrap(s + d)
        remote(ykv.at[ss], ykv_in.at[ss], ykv_s.at[d], ykv_r.at[ss], partner).wait_recv()
    for j in range(RING):
        for b in range(RING):
            rows = pl.ds((RING * j + b) * TOK, TOK)
            at = pl.ds(place_of(j, b) * TOK, TOK)
            total = ykv[s, rows, :].astype(F32)
            for d in (1, 2, 3):
                total += ykv_in[wrap(s + d), rows, :].astype(F32)
            whole = total.astype(BF16)
            kv[c, at, :] = jnp.where(first, rotate(whole.astype(F32), at), whole.astype(F32)).astype(BF16)
    kv_d2d = remote(kv.at[c], kv.at[c], d2d_s.at[2], d2d_r.at[2], partner)
    kv_d2d.start()
    remote(kv.at[oc], kv.at[oc], d2d_s.at[2], d2d_r.at[2], partner).wait_recv()

    h_copies, o_copies = [], []

    def attend(j):
        for d in (1, 2, 3):
            ss = wrap(s + d)
            remote(yq.at[j, ss], yq_in.at[j, ss], yq_s.at[j, d], yq_r.at[j, ss], partner).wait_recv()
        for b in range(RING):
            n = place_of(j, b)
            rows, at = pl.ds(b * TOK, TOK), pl.ds(n * TOK, TOK)
            total = yq[j, s, rows, :].astype(F32)
            for d in (1, 2, 3):
                total += yq_in[j, wrap(s + d), rows, :].astype(F32)
            q = jnp.concatenate(
                [rotate(total[:, :HEAD], at), rotate(total[:, HEAD:], at)], axis=0
            ).astype(BF16)
            keys = -(-(n + 1) * TOK // HEAD) * HEAD
            scores = lax.dot_general(
                q, kv[0, :keys, :], (((1,), (1,)), ((), ())), preferred_element_type=F32
            )
            row = lax.broadcasted_iota(jnp.int32, (2 * TOK, keys), 0)
            row = jnp.where(row >= TOK, row - TOK, row) + n * TOK
            col = lax.broadcasted_iota(jnp.int32, (2 * TOK, keys), 1)
            scores = jnp.where(col <= row, scores, -jnp.inf)
            top = jnp.max(scores, axis=1, keepdims=True)
            expo = jnp.exp2((scores - top) * EXP_SCALE)
            norm = jnp.sum(expo, axis=1, keepdims=True)
            head = jnp.dot(expo.astype(BF16), kv[1, :keys, :], preferred_element_type=F32) / norm
            hbuf[c, j, rows, :] = jnp.concatenate([head[:TOK], head[TOK:]], axis=1).astype(BF16)
        copy = remote(hbuf.at[c, j], hbuf.at[c, j], h_s.at[j], h_r.at[j], partner)
        copy.start()
        h_copies.append(copy)

    def project(j):
        remote(hbuf.at[oc, j], hbuf.at[oc, j], h_s.at[j], h_r.at[j], partner).wait_recv()
        r = jnp.dot(hbuf[0, j], wo2[0], preferred_element_type=F32)
        r += jnp.dot(hbuf[1, j], wo2[1], preferred_element_type=F32)
        obuf[j] = r.astype(BF16).reshape(RING, TOK, HALF)
        for d in (2, 1, 3):
            pp = wrap(p + d)
            b = jnp.where(first, wrap(pp - j), pp)
            copy = remote(
                obuf.at[j, b], o1_in.at[j, p], o1_s.at[j, d], o1_r.at[j, p], device(pp, s)
            )
            copy.start()
            o_copies.append(copy)

    def target(j):
        return jnp.where(first, wrap(p - j), wrap(p + j))

    def second(j):
        ss = target(j)
        return remote(o1_sum.at[j], o2_in.at[s], o2_s.at[j], o2_r.at[s], device(p, ss))

    def combine(j):
        total = obuf[j, jnp.where(first, wrap(p - j), p)].astype(F32)
        for d in (1, 2, 3):
            pp = wrap(p + d)
            remote(obuf.at[j, 0], o1_in.at[j, pp], o1_s.at[j, d], o1_r.at[j, pp], partner).wait_recv()
            total += o1_in[j, pp].astype(F32)
        o1_sum[j] = total.astype(BF16)

        @pl.when(target(j) != s)
        def _():
            second(j).start()

    attend(0)
    for j in range(1, RING):
        attend(j)
        project(j - 1)
        if j >= 2:
            combine(j - 2)
    project(RING - 1)
    combine(RING - 2)
    combine(RING - 1)

    kept = jnp.where(first, wrap(p - s), wrap(s - p))
    total = o1_sum[kept].astype(F32)
    for d in (1, 2, 3):
        ss = wrap(s + d)
        remote(o1_sum.at[0], o2_in.at[ss], o2_s.at[0], o2_r.at[ss], partner).wait_recv()
        total += o2_in[ss].astype(F32)
    low, high = total[: TOK // 2], total[TOK // 2 :]
    fin_out[...] = jnp.where(first, high, low).astype(BF16)
    fin_d2d = remote(fin_out, fin_in, d2d_s.at[3], d2d_r.at[3], partner)
    fin_d2d.start()
    out_ref[:, pl.ds(pl.multiple_of(c * HALF, HALF), HALF)] = jnp.where(first, low, high).astype(BF16)

    kv_d2d.wait_send()
    for copy in w_copies + x_copies + y_copies + h_copies + o_copies:
        copy.wait_send()
    for j in range(RING):

        @pl.when(target(j) != s)
        def _(j=j):
            second(j).wait_send()

    fin_d2d.wait()
    out_ref[:, pl.ds(pl.multiple_of(oc * HALF, HALF), HALF)] = fin_in[...]


def shards(hidden_in, query_weight, key_weight, value_projection_weight, output_weight, head_order, positions):
    heads = jnp.arange(head_order.shape[0], dtype=jnp.int32)
    inverse = jnp.sum(
        jnp.where(head_order[None, :] == heads[:, None], heads[None, :], 0), axis=1, dtype=jnp.int32
    )
    half = np.float32(ROPE_BASE) ** (
        np.float32(-2.0) * np.arange(HEAD // 2, dtype=np.float32) / np.float32(HEAD)
    )
    angles = positions.astype(F32)[:, None] * jnp.asarray(np.concatenate([half, half]))[None, :]
    vmem, dma = pltpu.VMEM, pltpu.SemaphoreType.DMA
    any_spec = pl.BlockSpec(memory_space=pl.ANY)
    vmem_spec = pl.BlockSpec(memory_space=vmem)
    return pl.pallas_call(
        kernel,
        out_shape=jax.ShapeDtypeStruct((TOK // 2, FEAT), BF16),
        in_specs=[any_spec] * 5 + [pl.BlockSpec(memory_space=pltpu.SMEM), vmem_spec],
        out_specs=vmem_spec,
        scratch_shapes=[
            vmem((2, TOK // 2, FEAT), BF16),
            vmem((RING, TOK, DEPTH), BF16),
            vmem((RING * RING, TOK, DEPTH), BF16),
            vmem((64, 128, HEAD), BF16),
            vmem((2, 128, 1024), BF16),
            vmem((2 * RING, 128, KV_COLS + Q_COLS), BF16),
            vmem((2 * RING, 128, KV_COLS + Q_COLS), BF16),
            vmem((2, 2 * HEAD, HALF), BF16),
            vmem((SPAN, HEAD), F32),
            vmem((SPAN, HEAD), F32),
            vmem((RING, SPAN, HEAD), BF16),
            vmem((RING, SPAN, HEAD), BF16),
            vmem((RING, RING, ROWS, 2 * HEAD), BF16),
            vmem((RING, RING, ROWS, 2 * HEAD), BF16),
            vmem((2, SPAN, HEAD), BF16),
            vmem((2, RING, ROWS, 2 * HEAD), BF16),
            vmem((RING, RING, TOK, HALF), BF16),
            vmem((RING, RING, TOK, HALF), BF16),
            vmem((RING, TOK, HALF), BF16),
            vmem((RING, TOK, HALF), BF16),
            vmem((TOK // 2, HALF), BF16),
            vmem((TOK // 2, HALF), BF16),
            dma((5,)), dma((4,)), dma((4,)),
            dma((2 * RING,)), dma((2 * RING,)),
            dma((RING,)), dma((RING * RING,)), dma((RING * RING,)),
            dma((RING,)), dma((RING,)), dma((RING, RING)), dma((RING, RING)),
            dma((RING,)), dma((RING,)),
            dma((RING, RING)), dma((RING, RING)), dma((RING,)), dma((RING,)),
        ],
        compiler_params=pltpu.CompilerParams(
            collective_id=0, has_side_effects=True, vmem_limit_bytes=56 << 20
        ),
        cost_estimate=pl.CostEstimate(flops=6 << 30, bytes_accessed=8 << 20, transcendentals=1 << 20),
    )(hidden_in, query_weight, key_weight, value_projection_weight, output_weight, inverse, angles)


def solution(mesh):
    return jax.shard_map(
        shards,
        mesh=mesh,
        in_specs=(
            P(("replica", "tensor"), None),
            P("tensor", None),
            P("tensor", None),
            P("tensor", None),
            P("tensor", None),
            P(),
            P("replica"),
        ),
        out_specs=P(("replica", "tensor"), None),
        check_vma=False,
    )
```

```python
import math

import jax
import jax.numpy as jnp
import numpy as np
from jax import lax
from jax.experimental import pallas as pl
from jax.experimental.pallas import tpu as pltpu
from jax.sharding import PartitionSpec as P

MESH = pl.DeviceIdType.MESH
F32, BF16 = jnp.float32, jnp.bfloat16

HEAD = 128
RING = 4
TOK = 48
ROWS = RING * TOK
CUT = 16
CHUNK = RING * RING * CUT
SPAN = RING * ROWS
FEAT = 4096
DEPTH = FEAT // RING
KV_COLS = RING * HEAD
Q_COLS = RING * 2 * HEAD
HALF = FEAT // 2
WIDE = HALF // 2
HEADS = 64
W_ROWS = 128
ROPE_BASE = 1000000.0
EXP_SCALE = math.log2(math.e) / math.sqrt(HEAD)


def kernel(
    x_hbm, wq_hbm, wk_hbm, wv_hbm, wo_hbm, order_ref, pos_ref, freq_ref,
    out_ref,
    xpair, xs, xall, wq, wkv, wsend, wall, wo2, inv_v, inv_s, cos_t, sin_t,
    ykv, ykv_in, yq, yq_in, kv, hbuf, obuf, f_in, o1_in, o1_sum, o2_in, fin_out, fin_in,
    loc_sem, d2d_s, d2d_r, w_s, w_r, z_s, z_r, x1_s, x2_s, x_r, ykv_s, ykv_r, yq_s, yq_r,
    kv_s, kv_r, h_s, h_r, f_s, f_r, o1_s, o1_r, o2_s, o2_r,
):
    t = lax.axis_index("tensor")
    z = lax.axis_index("replica")
    planes = lax.axis_size("replica")
    y, x, c = t // 8, (t // 2) % 4, t % 2
    first = c == 0
    p, s = jnp.where(first, x, y), jnp.where(first, y, x)
    oc = 1 - c
    part = z % 2

    def wrap(v):
        return lax.rem(v + 8, RING)

    def device(pp, ss):
        return jnp.where(first, 8 * ss + 2 * pp, 8 * pp + 2 * ss + 1)

    def slot(pp, ss):
        return jnp.where(first, RING * ss + pp, RING * pp + ss)

    def remote(src, dst, ss, rs, dev, dz=0):
        where = {"tensor": dev}
        if dz:
            where["replica"] = lax.rem(z + dz + planes, planes)
        return pltpu.make_async_remote_copy(
            src_ref=src, dst_ref=dst, send_sem=ss, recv_sem=rs,
            device_id=where, device_id_type=MESH,
        )

    partner = t + 1 - 2 * c

    barrier = pltpu.get_barrier_semaphore()

    def greet(dev, dz=0):
        where = {"tensor": dev}
        if dz:
            where["replica"] = lax.rem(z + dz + planes, planes)
        pl.semaphore_signal(barrier, inc=1, device_id=where, device_id_type=MESH)

    for d in range(1, RING):
        ring = device(wrap(p + d), s)
        greet(ring)
        greet(ring + 1 - 2 * c)
        greet(device(p, wrap(s + d)))
    greet(t, 1)
    greet(t, -1)
    greet(partner)

    own_x = pltpu.make_async_copy(x_hbm, xpair.at[c], loc_sem.at[0])
    own_q = pltpu.make_async_copy(wq, wq, loc_sem.at[1])
    own_k = pltpu.make_async_copy(wk_hbm, wkv.at[0], loc_sem.at[2])
    own_v = pltpu.make_async_copy(wv_hbm, wkv.at[1], loc_sem.at[3])
    own_o = pltpu.make_async_copy(
        wo_hbm.at[:, pl.ds(pl.multiple_of(c * HALF, HALF), HALF)], wo2.at[c], loc_sem.at[4]
    )

    def load_head(i, _):
        cols = pl.ds(pl.multiple_of(i * HEAD, HEAD), HEAD)
        pltpu.make_async_copy(wq_hbm.at[:, cols], wq.at[i], loc_sem.at[1]).start()
        return 0

    own_k.start()
    own_v.start()
    lax.fori_loop(0, HEADS, load_head, 0, unroll=8)
    own_x.start()
    own_o.start()

    lane = lax.broadcasted_iota(jnp.int32, (8, HEAD), 1)

    def invert(i, acc):
        return jnp.where(lane == order_ref[i], i, acc)

    inv_v[...] = lax.fori_loop(0, HEADS, invert, jnp.zeros((8, HEAD), jnp.int32), unroll=8)
    to_scalars = pltpu.make_async_copy(inv_v, inv_s, loc_sem.at[5])
    to_scalars.start()

    pl.semaphore_wait(barrier, 12)

    x_d2d = remote(x_hbm, xpair.at[c], d2d_s.at[0], d2d_r.at[0], partner)
    x_d2d.start()
    to_scalars.wait()
    own_k.wait()
    own_v.wait()
    own_q.wait()

    sends = []
    half_rows = W_ROWS // 2
    moved = pl.ds(pl.multiple_of(part * half_rows, half_rows), half_rows)
    brought = pl.ds(pl.multiple_of((1 - part) * half_rows, half_rows), half_rows)

    def weights(other, d):
        cc = jnp.where(other == 1, oc, c)
        cc_first = cc == 0
        pcc = jnp.where(cc_first, x, y)
        pp = wrap(pcc + d)
        own = other == 0 and d == 0
        rows = moved if d else pl.ds(0, W_ROWS)
        place = wall.at[2 * p + c] if own else wsend.at[RING * other + d]

        def fill(ss, _):
            tt = jnp.where(cc_first, 8 * ss + 2 * pp, 8 * pp + 2 * ss + 1)
            group = pl.multiple_of((tt // 4) * HEAD, HEAD)
            place[rows, pl.ds(pl.multiple_of(ss * HEAD, HEAD), HEAD)] = wkv[cc, rows, pl.ds(group, HEAD)]
            for i in range(2):
                at = pl.multiple_of(KV_COLS + (2 * ss + i) * HEAD, HEAD)
                place[rows, pl.ds(at, HEAD)] = wq[inv_s[0, 2 * tt + i], rows]
            return 0

        lax.fori_loop(0, RING, fill, 0)
        if not own:
            dev = jnp.where(cc_first, 8 * y + 2 * pp, 8 * pp + 2 * x + 1)
            copy = remote(
                place.at[rows], wall.at[2 * pcc + c, rows],
                w_s.at[RING * other + d], w_r.at[2 * pcc + c], dev,
            )
            copy.start()
            sends.append(copy)

    for d in (1, 3, 2):
        weights(0, d)

    own_x.wait()
    remote(x_hbm, xpair.at[oc], d2d_s.at[0], d2d_r.at[0], partner).wait_recv()
    mine = slot(p, s)
    for d in (1, 3, 2, 0):
        ss = wrap(s + d)
        for pp in range(RING):
            feat = pl.multiple_of(
                jnp.where(first, DEPTH * ss + 256 * pp, DEPTH * pp + 256 * ss), 256
            )
            rows = jnp.concatenate(
                [xpair[0, :, pl.ds(feat, 256)].astype(F32), xpair[1, :, pl.ds(feat, 256)].astype(F32)],
                axis=0,
            ).astype(BF16)
            if d == 0:
                xall[mine, :, 256 * pp : 256 * pp + 256] = rows
            else:
                xs[d, :, 256 * pp : 256 * pp + 256] = rows
        if d:
            copy = remote(xs.at[d], xall.at[mine], x1_s.at[d], x_r.at[mine], device(p, ss))
            copy.start()
            sends.append(copy)

    for d in (1, 3, 2):
        weights(1, d)
    weights(1, 0)
    weights(0, 0)
    x_d2d.wait_send()
    wo_d2d = remote(
        wo_hbm.at[:, pl.ds(pl.multiple_of(oc * HALF, HALF), HALF)], wo2.at[c],
        d2d_s.at[1], d2d_r.at[1], partner,
    )
    wo_d2d.start()

    def arrived(m):
        remote(xall.at[m], xall.at[m], x1_s.at[0], x_r.at[m], partner).wait_recv()

    def from_plane(e):
        for other in (0, 1):
            k = 2 * wrap(p + e) + (oc if other else c)
            here = wall.at[k, moved]
            remote(here, here, w_s.at[0], w_r.at[k], partner).wait_recv()
            copy = remote(here, here, z_s.at[k], z_r.at[k], t, -1 if other else 1)
            copy.start()
            sends.append(copy)

    def forward(d):
        m = slot(p, wrap(s + d))
        if d:
            arrived(m)
        for e in (1, 3, 2):
            copy = remote(
                xall.at[m], xall.at[m], x2_s.at[RING * e + d], x_r.at[m], device(wrap(p + e), s)
            )
            copy.start()
            sends.append(copy)

    from_plane(1)
    from_plane(3)
    for d in range(RING):
        forward(d)
    from_plane(2)

    eye = lax.broadcasted_iota(jnp.int32, (HEAD, HEAD), 0) == lax.broadcasted_iota(
        jnp.int32, (HEAD, HEAD), 1
    )
    sign = jnp.where(lax.broadcasted_iota(jnp.int32, (HEAD, HEAD), 1) < HEAD // 2, -1.0, 1.0)

    def table(n, _):
        at = pl.ds(pl.multiple_of(n * HEAD, HEAD), HEAD)
        line = pos_ref[at].astype(F32)
        column = jnp.sum(jnp.where(eye, line[None, :], 0.0), axis=1, keepdims=True)
        ang = column * freq_ref[...]
        cos_t[at, :] = jnp.cos(ang)
        sin_t[at, :] = jnp.sin(ang) * sign
        return 0

    lax.fori_loop(0, SPAN // HEAD, table, 0)

    own_o.wait()
    wo_d2d.wait()
    k = 2 * p + oc
    remote(wall.at[k], wall.at[k], w_s.at[0], w_r.at[k], partner).wait_recv()
    for e in (1, 3, 2):
        for other in (0, 1):
            k = 2 * wrap(p + e) + (oc if other else c)
            there = wall.at[k, brought]
            remote(there, there, z_s.at[k], z_r.at[k], partner).wait_recv()
    for e in (1, 3, 2):
        for ss in range(RING):
            arrived(slot(wrap(p + e), ss))

    kv_sends = []
    for j in range(RING):
        at = pl.ds(j * ROWS, ROWS)
        r = jnp.dot(
            xall[RING * j : RING * j + RING].reshape(ROWS, DEPTH),
            wall[:, :, :KV_COLS].reshape(DEPTH, KV_COLS),
            preferred_element_type=F32,
        ).astype(BF16)
        for ss in range(RING):
            ykv[ss, at, :] = r[:, ss * HEAD : (ss + 1) * HEAD]
        for d in (2, 1, 3):
            ss = wrap(s + d)
            copy = remote(
                ykv.at[ss, at], ykv_in.at[s, at], ykv_s.at[j, d], ykv_r.at[j, s], device(p, ss)
            )
            copy.start()
            kv_sends.append(copy)

    q_sends = [[], [], []]

    def queries(j):
        r = jnp.dot(
            xall[:, CUT * j : CUT * j + CUT].reshape(CHUNK, DEPTH),
            wall[:, :, KV_COLS:].reshape(DEPTH, Q_COLS),
            preferred_element_type=F32,
        ).astype(BF16)
        for ss in range(RING):
            yq[j, ss] = r[:, ss * 2 * HEAD : (ss + 1) * 2 * HEAD]

    def send_queries(j):
        for d in (2, 1, 3):
            ss = wrap(s + d)
            copy = remote(yq.at[j, ss], yq_in.at[j, s], yq_s.at[j, d], yq_r.at[j, s], device(p, ss))
            copy.start()
            q_sends[j].append(copy)

    queries(0)
    send_queries(0)
    queries(1)
    queries(2)
    for copy in kv_sends:
        copy.wait_send()
    send_queries(1)

    for j in range(RING):
        at = pl.ds(j * ROWS, ROWS)
        total = ykv[s, at, :].astype(F32)
        for d in (1, 2, 3):
            ss = wrap(s + d)
            remote(
                ykv.at[ss, at], ykv_in.at[ss, at], ykv_s.at[j, d], ykv_r.at[j, ss], partner
            ).wait_recv()
            total += ykv_in[ss, at, :].astype(F32)
        whole = total.astype(BF16).astype(F32)
        turned = whole * cos_t[at, :] + pltpu.roll(whole, HEAD // 2, 1) * sin_t[at, :]
        kv[c, at, :] = jnp.where(first, turned, whole).astype(BF16)
        copy = remote(kv.at[c, at], kv.at[c, at], kv_s.at[j], kv_r.at[j], partner)
        copy.start()
        sends.append(copy)
    for copy in q_sends[0]:
        copy.wait_send()
    send_queries(2)
    for j in range(RING):
        at = pl.ds(j * ROWS, ROWS)
        remote(kv.at[oc, at], kv.at[oc, at], kv_s.at[j], kv_r.at[j], partner).wait_recv()

    def attend(j):
        for d in (1, 2, 3):
            ss = wrap(s + d)
            remote(yq.at[j, ss], yq_in.at[j, ss], yq_s.at[j, d], yq_r.at[j, ss], partner).wait_recv()
        for b in range(RING):
            rows = pl.ds(b * ROWS // 3, ROWS // 3)
            total = yq[j, s, rows, :].astype(F32)
            for d in (1, 2, 3):
                total += yq_in[j, wrap(s + d), rows, :].astype(F32)
            cos = jnp.concatenate(
                [cos_t[pl.ds(ROWS * b + TOK * i + CUT * j, CUT), :] for i in range(RING)], axis=0
            )
            sin = jnp.concatenate(
                [sin_t[pl.ds(ROWS * b + TOK * i + CUT * j, CUT), :] for i in range(RING)], axis=0
            )
            q = jnp.concatenate(
                [
                    v * cos + pltpu.roll(v, HEAD // 2, 1) * sin
                    for v in (total[:, :HEAD], total[:, HEAD:])
                ],
                axis=0,
            ).astype(BF16)
            keys = -(-(b + 1) * ROWS // HEAD) * HEAD
            scores = lax.dot_general(
                q, kv[0, :keys, :], (((1,), (1,)), ((), ())), preferred_element_type=F32
            )
            row = lax.broadcasted_iota(jnp.int32, (2 * ROWS // 3, keys), 0) % (ROWS // 3)
            row = ROWS * b + TOK * (row // CUT) + CUT * j + row % CUT
            col = lax.broadcasted_iota(jnp.int32, (2 * ROWS // 3, keys), 1)
            scores = jnp.where(col <= row, scores, -jnp.inf)
            top = jnp.max(scores, axis=1, keepdims=True)
            expo = jnp.exp2((scores - top) * EXP_SCALE)
            norm = jnp.sum(expo, axis=1, keepdims=True)
            head = jnp.dot(expo.astype(BF16), kv[1, :keys, :], preferred_element_type=F32) / norm
            hbuf[c, j, rows, :] = jnp.concatenate(
                [head[: ROWS // 3], head[ROWS // 3 :]], axis=1
            ).astype(BF16)
        copy = remote(hbuf.at[c, j], hbuf.at[c, j], h_s.at[j], h_r.at[j], partner)
        copy.start()
        sends.append(copy)

    def project(k):
        j, cols = k // 2, pl.ds((k % 2) * WIDE, WIDE)
        if k % 2 == 0:
            remote(hbuf.at[oc, j], hbuf.at[oc, j], h_s.at[j], h_r.at[j], partner).wait_recv()
        r = jnp.dot(hbuf[0, j], wo2[0, :, cols], preferred_element_type=F32)
        r += jnp.dot(hbuf[1, j], wo2[1, :, cols], preferred_element_type=F32)
        r = r.astype(BF16)
        for n in range(RING * RING):
            i, b = n // RING, n % RING
            obuf[k, jnp.where(first, b, i), jnp.where(first, i, b)] = r[CUT * n : CUT * n + CUT]
        far = wrap(p + 2)
        for d, i in ((1, 0), (3, 1)):
            copy = remote(
                obuf.at[k, far, pl.ds(2 * i, 2)], f_in.at[k, i], f_s.at[k, i], f_r.at[k, i],
                device(wrap(p + d), s),
            )
            copy.start()
            sends.append(copy)

    def fold(k):
        for d, i in ((1, 0), (3, 1)):
            near = wrap(p + d)
            remote(f_in.at[k, i], f_in.at[k, i], f_s.at[k, i], f_r.at[k, i], partner).wait_recv()
            half = pl.ds(2 * i, 2)
            obuf[k, near, half] = (
                obuf[k, near, half].astype(F32) + f_in[k, i].astype(F32)
            ).astype(BF16)
            copy = remote(
                obuf.at[k, near], o1_in.at[k, i], o1_s.at[k, i], o1_r.at[k, i], device(near, s)
            )
            copy.start()
            sends.append(copy)

    def combine(k):
        total = obuf[k, p].astype(F32)
        for i in range(2):
            remote(o1_in.at[k, i], o1_in.at[k, i], o1_s.at[k, i], o1_r.at[k, i], partner).wait_recv()
            total += o1_in[k, i].astype(F32)
        o1_sum[k] = total.astype(BF16)
        for d in (2, 1, 3):
            ss = wrap(s + d)
            copy = remote(
                o1_sum.at[k, ss], o2_in.at[k, s], o2_s.at[k, d], o2_r.at[k, s], device(p, ss)
            )
            copy.start()
            sends.append(copy)

    attend(0)
    attend(1)
    project(0)
    project(1)
    attend(2)
    project(2)
    fold(0)
    project(3)
    fold(1)
    project(4)
    fold(2)
    combine(0)
    project(5)
    fold(3)
    combine(1)
    fold(4)
    combine(2)
    fold(5)
    for k in (3, 4, 5):
        combine(k)

    def finish(k):
        total = o1_sum[k, s].astype(F32)
        for d in (1, 2, 3):
            ss = wrap(s + d)
            remote(o1_sum.at[k, 0], o2_in.at[k, ss], o2_s.at[k, d], o2_r.at[k, ss], partner).wait_recv()
            total += o2_in[k, ss].astype(F32)
        return total

    done = [finish(k) for k in range(6)]
    total = jnp.concatenate(
        [jnp.concatenate([done[2 * j], done[2 * j + 1]], axis=1) for j in range(3)], axis=0
    )
    low, high = total[: TOK // 2], total[TOK // 2 :]
    fin_out[...] = jnp.where(first, high, low).astype(BF16)
    fin_d2d = remote(fin_out, fin_in, d2d_s.at[2], d2d_r.at[2], partner)
    fin_d2d.start()
    out_ref[:, pl.ds(pl.multiple_of(c * HALF, HALF), HALF)] = jnp.where(first, low, high).astype(BF16)

    for copy in sends + q_sends[1] + q_sends[2]:
        copy.wait_send()
    fin_d2d.wait()
    out_ref[:, pl.ds(pl.multiple_of(oc * HALF, HALF), HALF)] = fin_in[...]


def shards(hidden_in, query_weight, key_weight, value_projection_weight, output_weight, head_order, positions):
    half = np.float32(ROPE_BASE) ** (
        np.float32(-2.0) * np.arange(HEAD // 2, dtype=np.float32) / np.float32(HEAD)
    )
    freq = jnp.asarray(np.concatenate([half, half])[None, :])
    vmem, dma = pltpu.VMEM, pltpu.SemaphoreType.DMA
    any_spec = pl.BlockSpec(memory_space=pl.ANY)
    vmem_spec = pl.BlockSpec(memory_space=vmem)
    return pl.pallas_call(
        kernel,
        out_shape=jax.ShapeDtypeStruct((TOK // 2, FEAT), BF16),
        in_specs=[any_spec] * 5 + [pl.BlockSpec(memory_space=pltpu.SMEM), vmem_spec, vmem_spec],
        out_specs=vmem_spec,
        scratch_shapes=[
            vmem((2, TOK // 2, FEAT), BF16),
            vmem((RING, TOK, DEPTH), BF16),
            vmem((RING * RING, TOK, DEPTH), BF16),
            vmem((HEADS, W_ROWS, HEAD), BF16),
            vmem((2, W_ROWS, 1024), BF16),
            vmem((2 * RING, W_ROWS, KV_COLS + Q_COLS), BF16),
            vmem((2 * RING, W_ROWS, KV_COLS + Q_COLS), BF16),
            vmem((2, 2 * HEAD, HALF), BF16),
            vmem((8, HEAD), jnp.int32),
            pltpu.SMEM((8, HEAD), jnp.int32),
            vmem((SPAN, HEAD), F32),
            vmem((SPAN, HEAD), F32),
            vmem((RING, SPAN, HEAD), BF16),
            vmem((RING, SPAN, HEAD), BF16),
            vmem((3, RING, CHUNK, 2 * HEAD), BF16),
            vmem((3, RING, CHUNK, 2 * HEAD), BF16),
            vmem((2, SPAN, HEAD), BF16),
            vmem((2, 3, CHUNK, 2 * HEAD), BF16),
            vmem((6, RING, RING, CUT, WIDE), BF16),
            vmem((6, 2, 2, CUT, WIDE), BF16),
            vmem((6, 2, RING, CUT, WIDE), BF16),
            vmem((6, RING, CUT, WIDE), BF16),
            vmem((6, RING, CUT, WIDE), BF16),
            vmem((TOK // 2, HALF), BF16),
            vmem((TOK // 2, HALF), BF16),
            dma((6,)), dma((3,)), dma((3,)),
            dma((2 * RING,)), dma((2 * RING,)), dma((2 * RING,)), dma((2 * RING,)),
            dma((RING,)), dma((RING * RING,)), dma((RING * RING,)),
            dma((RING, RING)), dma((RING, RING)), dma((3, RING)), dma((3, RING)),
            dma((RING,)), dma((RING,)), dma((3,)), dma((3,)),
            dma((6, 2)), dma((6, 2)), dma((6, 2)), dma((6, 2)), dma((6, RING)), dma((6, RING)),
        ],
        compiler_params=pltpu.CompilerParams(
            collective_id=0, has_side_effects=True, vmem_limit_bytes=56 << 20
        ),
        cost_estimate=pl.CostEstimate(flops=6 << 30, bytes_accessed=8 << 20, transcendentals=1 << 20),
    )(hidden_in, query_weight, key_weight, value_projection_weight, output_weight, head_order, positions, freq)


def solution(mesh):
    return jax.shard_map(
        shards,
        mesh=mesh,
        in_specs=(
            P(("replica", "tensor"), None),
            P("tensor", None),
            P("tensor", None),
            P("tensor", None),
            P("tensor", None),
            P(),
            P("replica"),
        ),
        out_specs=P(("replica", "tensor"), None),
        check_vma=False,
    )
```

```python
import math

import jax
import jax.numpy as jnp
import numpy as np
from jax import lax
from jax.experimental import pallas as pl
from jax.experimental.pallas import tpu as pltpu
from jax.sharding import PartitionSpec as P

MESH = pl.DeviceIdType.MESH
F32, BF16 = jnp.float32, jnp.bfloat16

HEAD = 128
RING = 4
TOK = 48
ROWS = RING * TOK
SPAN = RING * ROWS
FEAT = 4096
DEPTH = FEAT // RING
KV_COLS = RING * HEAD
Q_COLS = RING * 2 * HEAD
HALF = FEAT // 2
WIDE = HALF // 2
PART = HALF // RING
HEADS = 64
W_ROWS = 128
ROPE_BASE = 1000000.0
EXP_SCALE = math.log2(math.e) / math.sqrt(HEAD)


def kernel(
    x_hbm, wq_hbm, wk_hbm, wv_hbm, wo_hbm, order_ref, pos_ref, freq_ref,
    out_ref,
    xpair, xs, xall, wq, wkv, wsend, wall, wo2, inv_v, inv_s, cos_t, sin_t,
    ykv, ykv_in, yq, yq_in, kv, hbuf, obuf, f_in, o1_in, o1_sum, o2_in, fin_out, fin_in,
    loc_sem, d2d_s, d2d_r, w_s, w_r, z_s, z_r, x1_s, x2_s, x_r, ykv_s, ykv_r, yq_s, yq_r,
    kv_s, kv_r, h_s, h_r, f_s, f_r, o1_s, o1_r, o2_s, o2_r, fin_s, fin_r,
):
    t = lax.axis_index("tensor")
    z = lax.axis_index("replica")
    planes = lax.axis_size("replica")
    y, x, c = t // 8, (t // 2) % 4, t % 2
    first = c == 0
    p, s = jnp.where(first, x, y), jnp.where(first, y, x)
    oc = 1 - c
    part = z % 2

    def wrap(v):
        return lax.rem(v + 8, RING)

    def device(pp, ss):
        return jnp.where(first, 8 * ss + 2 * pp, 8 * pp + 2 * ss + 1)

    def slot(pp, ss):
        return jnp.where(first, RING * ss + pp, RING * pp + ss)

    def remote(src, dst, ss, rs, dev, dz=0):
        where = {"tensor": dev}
        if dz:
            where["replica"] = lax.rem(z + dz + planes, planes)
        return pltpu.make_async_remote_copy(
            src_ref=src, dst_ref=dst, send_sem=ss, recv_sem=rs,
            device_id=where, device_id_type=MESH,
        )

    partner = t + 1 - 2 * c

    barrier = pltpu.get_barrier_semaphore()

    def greet(dev, dz=0):
        where = {"tensor": dev}
        if dz:
            where["replica"] = lax.rem(z + dz + planes, planes)
        pl.semaphore_signal(barrier, inc=1, device_id=where, device_id_type=MESH)

    for d in range(1, RING):
        ring = device(wrap(p + d), s)
        greet(ring)
        greet(ring + 1 - 2 * c)
        greet(device(p, wrap(s + d)))
    greet(t, 1)
    greet(t, -1)
    greet(partner)

    @pl.when(first)
    def _():
        for d in range(1, RING):
            greet(8 * wrap(y + d) + 2 * x + 1)

    own_x = pltpu.make_async_copy(x_hbm, xpair.at[c], loc_sem.at[0])
    own_q = pltpu.make_async_copy(wq, wq, loc_sem.at[1])
    own_k = pltpu.make_async_copy(wk_hbm, wkv.at[0], loc_sem.at[2])
    own_v = pltpu.make_async_copy(wv_hbm, wkv.at[1], loc_sem.at[3])
    own_o = pltpu.make_async_copy(
        wo_hbm.at[:, pl.ds(pl.multiple_of(c * HALF, HALF), HALF)], wo2.at[c], loc_sem.at[4]
    )

    def load_head(i, _):
        cols = pl.ds(pl.multiple_of(i * HEAD, HEAD), HEAD)
        pltpu.make_async_copy(wq_hbm.at[:, cols], wq.at[i], loc_sem.at[1]).start()
        return 0

    own_k.start()
    own_v.start()
    lax.fori_loop(0, HEADS, load_head, 0, unroll=8)
    own_x.start()
    own_o.start()

    lane = lax.broadcasted_iota(jnp.int32, (8, HEAD), 1)

    def invert(i, acc):
        return jnp.where(lane == order_ref[i], i, acc)

    inv_v[...] = lax.fori_loop(0, HEADS, invert, jnp.zeros((8, HEAD), jnp.int32), unroll=8)
    to_scalars = pltpu.make_async_copy(inv_v, inv_s, loc_sem.at[5])
    to_scalars.start()

    pl.semaphore_wait(barrier, 12 + 3 * c)

    x_d2d = remote(x_hbm, xpair.at[c], d2d_s.at[0], d2d_r.at[0], partner)
    x_d2d.start()
    to_scalars.wait()
    own_k.wait()
    own_v.wait()
    own_q.wait()

    sends = []
    half_rows = W_ROWS // 2
    moved = pl.ds(pl.multiple_of(part * half_rows, half_rows), half_rows)
    brought = pl.ds(pl.multiple_of((1 - part) * half_rows, half_rows), half_rows)

    def weights(other, d):
        cc = jnp.where(other == 1, oc, c)
        cc_first = cc == 0
        pcc = jnp.where(cc_first, x, y)
        pp = wrap(pcc + d)
        own = other == 0 and d == 0
        rows = moved if d else pl.ds(0, W_ROWS)
        place = wall.at[2 * p + c] if own else wsend.at[RING * other + d]

        def fill(ss, _):
            tt = jnp.where(cc_first, 8 * ss + 2 * pp, 8 * pp + 2 * ss + 1)
            group = pl.multiple_of((tt // 4) * HEAD, HEAD)
            place[rows, pl.ds(pl.multiple_of(ss * HEAD, HEAD), HEAD)] = wkv[cc, rows, pl.ds(group, HEAD)]
            for i in range(2):
                at = pl.multiple_of(KV_COLS + (2 * ss + i) * HEAD, HEAD)
                place[rows, pl.ds(at, HEAD)] = wq[inv_s[0, 2 * tt + i], rows]
            return 0

        lax.fori_loop(0, RING, fill, 0)
        if not own:
            dev = jnp.where(cc_first, 8 * y + 2 * pp, 8 * pp + 2 * x + 1)
            copy = remote(
                place.at[rows], wall.at[2 * pcc + c, rows],
                w_s.at[RING * other + d], w_r.at[2 * pcc + c], dev,
            )
            sends.append(copy)
            return copy

    near = [weights(other, d) for d in (1, 3) for other in (0, 1)]
    for copy in near:
        copy.start()

    own_x.wait()
    remote(x_hbm, xpair.at[oc], d2d_s.at[0], d2d_r.at[0], partner).wait_recv()
    mine = slot(p, s)
    for d in (1, 3, 2, 0):
        ss = wrap(s + d)
        for pp in range(RING):
            feat = pl.multiple_of(
                jnp.where(first, DEPTH * ss + 256 * pp, DEPTH * pp + 256 * ss), 256
            )
            rows = jnp.concatenate(
                [xpair[0, :, pl.ds(feat, 256)].astype(F32), xpair[1, :, pl.ds(feat, 256)].astype(F32)],
                axis=0,
            ).astype(BF16)
            if d == 0:
                xall[mine, :, 256 * pp : 256 * pp + 256] = rows
            else:
                xs[d, :, 256 * pp : 256 * pp + 256] = rows
        if d:
            copy = remote(xs.at[d], xall.at[mine], x1_s.at[d], x_r.at[mine], device(p, ss))
            copy.start()
            sends.append(copy)

    far = [weights(other, 2) for other in (0, 1)]
    weights(1, 0).start()
    weights(0, 0)
    x_d2d.wait_send()
    wo_d2d = remote(
        wo_hbm.at[:, pl.ds(pl.multiple_of(oc * HALF, HALF), HALF)], wo2.at[c],
        d2d_s.at[1], d2d_r.at[1], partner,
    )
    wo_d2d.start()

    def arrived(m):
        remote(xall.at[m], xall.at[m], x1_s.at[0], x_r.at[m], partner).wait_recv()

    def from_plane(e):
        for other in (0, 1):
            k = 2 * wrap(p + e) + (oc if other else c)
            here = wall.at[k, moved]
            remote(here, here, w_s.at[0], w_r.at[k], partner).wait_recv()
            copy = remote(here, here, z_s.at[k], z_r.at[k], t, -1 if other else 1)
            copy.start()
            sends.append(copy)

    def forward(d):
        m = slot(p, wrap(s + d))
        if d:
            arrived(m)
        for e in (1, 3, 2):
            copy = remote(
                xall.at[m], xall.at[m], x2_s.at[RING * e + d], x_r.at[m], device(wrap(p + e), s)
            )
            copy.start()
            sends.append(copy)

    eye = lax.broadcasted_iota(jnp.int32, (HEAD, HEAD), 0) == lax.broadcasted_iota(
        jnp.int32, (HEAD, HEAD), 1
    )
    sign = jnp.where(lax.broadcasted_iota(jnp.int32, (HEAD, HEAD), 1) < HEAD // 2, -1.0, 1.0)

    def table(n, _):
        at = pl.ds(pl.multiple_of(n * HEAD, HEAD), HEAD)
        line = pos_ref[at].astype(F32)
        column = jnp.sum(jnp.where(eye, line[None, :], 0.0), axis=1, keepdims=True)
        ang = column * freq_ref[...]
        cos_t[at, :] = jnp.cos(ang)
        sin_t[at, :] = jnp.sin(ang) * sign
        return 0

    lax.fori_loop(0, SPAN // HEAD, table, 0)

    for copy in near:
        copy.wait_send()
        sends.remove(copy)
    for copy in far:
        copy.start()
    from_plane(1)
    from_plane(3)
    for d in range(RING):
        forward(d)
    from_plane(2)
    own_o.wait()
    wo_d2d.wait()
    k = 2 * p + oc
    remote(wall.at[k], wall.at[k], w_s.at[0], w_r.at[k], partner).wait_recv()
    for e in (1, 3, 2):
        for other in (0, 1):
            k = 2 * wrap(p + e) + (oc if other else c)
            there = wall.at[k, brought]
            remote(there, there, z_s.at[k], z_r.at[k], partner).wait_recv()
    for e in (1, 3, 2):
        for ss in range(RING):
            arrived(slot(wrap(p + e), ss))

    q_sends = []

    def partial(i):
        at = pl.ds(i * ROWS, ROWS)
        r = jnp.dot(
            xall[RING * i : RING * i + RING].reshape(ROWS, DEPTH),
            wall[...].reshape(DEPTH, KV_COLS + Q_COLS),
            preferred_element_type=F32,
        ).astype(BF16)
        for ss in range(RING):
            ykv[ss, at, :] = r[:, ss * HEAD : (ss + 1) * HEAD]
            yq[i, ss] = r[:, KV_COLS + ss * 2 * HEAD : KV_COLS + (ss + 1) * 2 * HEAD]

    def send_kv(i):
        at = pl.ds(i * ROWS, ROWS)
        for d in (2, 1, 3):
            ss = wrap(s + d)
            copy = remote(
                ykv.at[ss, at], ykv_in.at[s, at], ykv_s.at[i, d], ykv_r.at[i, s], device(p, ss)
            )
            copy.start()
            sends.append(copy)

    def send_q(i):
        group = []
        for d in (2, 1, 3):
            ss = wrap(s + d)
            copy = remote(yq.at[i, ss], yq_in.at[i, s], yq_s.at[i, d], yq_r.at[i, s], device(p, ss))
            copy.start()
            group.append(copy)
        q_sends.append(group)

    def sent_q(i):
        for copy in q_sends[i]:
            copy.wait_send()

    def gather_kv(i):
        at = pl.ds(i * ROWS, ROWS)
        total = ykv[s, at, :].astype(F32)
        for d in (1, 2, 3):
            ss = wrap(s + d)
            remote(
                ykv.at[ss, at], ykv_in.at[ss, at], ykv_s.at[i, d], ykv_r.at[i, ss], partner
            ).wait_recv()
            total += ykv_in[ss, at, :].astype(F32)
        whole = total.astype(BF16).astype(F32)
        turned = whole * cos_t[at, :] + pltpu.roll(whole, HEAD // 2, 1) * sin_t[at, :]
        kv[c, at, :] = jnp.where(first, turned, whole).astype(BF16)
        copy = remote(kv.at[c, at], kv.at[c, at], kv_s.at[i], kv_r.at[i], partner)
        copy.start()
        sends.append(copy)

    def attend(i):
        at = pl.ds(i * ROWS, ROWS)
        remote(kv.at[oc, at], kv.at[oc, at], kv_s.at[i], kv_r.at[i], partner).wait_recv()
        total = yq[i, s].astype(F32)
        for d in (1, 2, 3):
            ss = wrap(s + d)
            remote(yq.at[i, ss], yq_in.at[i, ss], yq_s.at[i, d], yq_r.at[i, ss], partner).wait_recv()
            total += yq_in[i, ss].astype(F32)
        keys = (i + 1) * ROWS
        row = i * ROWS + lax.broadcasted_iota(jnp.int32, (ROWS, keys), 0)
        seen = lax.broadcasted_iota(jnp.int32, (ROWS, keys), 1) <= row
        for h in range(2):
            v = total[:, h * HEAD : (h + 1) * HEAD]
            q = (v * cos_t[at, :] + pltpu.roll(v, HEAD // 2, 1) * sin_t[at, :]).astype(BF16)
            scores = lax.dot_general(
                q, kv[0, :keys, :], (((1,), (1,)), ((), ())), preferred_element_type=F32
            )
            scores = jnp.where(seen, scores, -jnp.inf)
            top = jnp.max(scores, axis=1, keepdims=True)
            expo = jnp.exp2((scores - top) * EXP_SCALE)
            norm = jnp.sum(expo, axis=1, keepdims=True)
            head = jnp.dot(expo.astype(BF16), kv[1, :keys, :], preferred_element_type=F32) / norm
            hbuf[c, i, :, h * HEAD : (h + 1) * HEAD] = head.astype(BF16)
        copy = remote(hbuf.at[c, i], hbuf.at[c, i], h_s.at[i], h_r.at[i], partner)
        copy.start()
        sends.append(copy)

    def project(i):
        remote(hbuf.at[oc, i], hbuf.at[oc, i], h_s.at[i], h_r.at[i], partner).wait_recv()
        far_place = wrap(p + 2)
        for w in range(2):
            cols = pl.ds(w * WIDE, WIDE)
            r = jnp.dot(hbuf[0, i], wo2[0, :, cols], preferred_element_type=F32)
            r += jnp.dot(hbuf[1, i], wo2[1, :, cols], preferred_element_type=F32)
            r = r.astype(BF16)
            for b in range(RING):
                for v in range(2):
                    g = 2 * w + v
                    obuf[i, jnp.where(first, b, g), jnp.where(first, g, b)] = r[
                        b * TOK : (b + 1) * TOK, v * PART : (v + 1) * PART
                    ]
        for d, w in ((1, 0), (3, 1)):
            copy = remote(
                obuf.at[i, far_place, pl.ds(2 * w, 2)], f_in.at[i, w], f_s.at[i, w], f_r.at[i, w],
                device(wrap(p + d), s),
            )
            copy.start()
            sends.append(copy)

    def fold(i):
        for d, w in ((1, 0), (3, 1)):
            place, half = wrap(p + d), pl.ds(2 * w, 2)
            remote(f_in.at[i, w], f_in.at[i, w], f_s.at[i, w], f_r.at[i, w], partner).wait_recv()
            obuf[i, place, half] = (
                obuf[i, place, half].astype(F32) + f_in[i, w].astype(F32)
            ).astype(BF16)
            copy = remote(
                obuf.at[i, place], o1_in.at[i, w], o1_s.at[i, w], o1_r.at[i, w], device(place, s)
            )
            copy.start()
            sends.append(copy)

    def combine(i):
        total = obuf[i, p].astype(F32)
        for w in range(2):
            remote(o1_in.at[i, w], o1_in.at[i, w], o1_s.at[i, w], o1_r.at[i, w], partner).wait_recv()
            total += o1_in[i, w].astype(F32)
        o1_sum[i] = total.astype(BF16)
        for d in (2, 1, 3):
            ss = wrap(s + d)
            copy = remote(
                o1_sum.at[i, ss], o2_in.at[i, s], o2_s.at[i, d], o2_r.at[i, s], device(p, ss)
            )
            copy.start()
            sends.append(copy)

    def final(i, core):
        return remote(
            fin_out.at[i, core], fin_in.at[c, y], fin_s.at[i, core], fin_r.at[c, y],
            8 * i + 2 * x + core,
        )

    def finish(i):
        total = o1_sum[i, s].astype(F32)
        for d in (1, 2, 3):
            ss = wrap(s + d)
            remote(o1_sum.at[i, 0], o2_in.at[i, ss], o2_s.at[i, d], o2_r.at[i, ss], partner).wait_recv()
            total += o2_in[i, ss].astype(F32)
        for core in range(2):
            rows = total[core * (TOK // 2) : (core + 1) * (TOK // 2)].astype(BF16)
            fin_out[i, core] = rows
            mine_now = jnp.logical_and(y == i, c == core)

            @pl.when(mine_now)
            def _(rows=rows):
                fin_in[c, y] = rows

            @pl.when(jnp.logical_not(mine_now))
            def _(core=core):
                final(i, core).start()

    partial(0)
    send_kv(0)
    send_q(0)
    partial(1)
    send_kv(1)
    send_q(1)
    partial(2)
    send_kv(2)
    partial(3)
    send_kv(3)
    gather_kv(0)
    sent_q(0)
    send_q(2)
    gather_kv(1)
    sent_q(1)
    send_q(3)
    attend(0)
    gather_kv(2)
    attend(1)
    gather_kv(3)
    project(0)
    project(1)
    attend(2)
    fold(0)
    attend(3)
    fold(1)
    project(2)
    project(3)
    combine(0)
    fold(2)
    combine(1)
    fold(3)
    finish(0)
    combine(2)
    finish(1)
    combine(3)
    finish(2)
    finish(3)

    sent_q(2)
    sent_q(3)
    for copy in sends:
        copy.wait_send()
    for i in range(RING):
        for core in range(2):

            @pl.when(jnp.logical_or(y != i, c != core))
            def _(i=i, core=core):
                final(i, core).wait_send()

    for cc in range(2):
        for yy in range(RING):

            @pl.when(jnp.logical_or(y != yy, c != cc))
            def _(cc=cc, yy=yy):
                remote(
                    fin_out.at[0, 0], fin_in.at[cc, yy], fin_s.at[0, 0], fin_r.at[cc, yy], partner
                ).wait_recv()

            col = cc * HALF + yy * PART
            out_ref[:, col : col + PART] = fin_in[cc, yy]


def shards(hidden_in, query_weight, key_weight, value_projection_weight, output_weight, head_order, positions):
    half = np.float32(ROPE_BASE) ** (
        np.float32(-2.0) * np.arange(HEAD // 2, dtype=np.float32) / np.float32(HEAD)
    )
    freq = jnp.asarray(np.concatenate([half, half])[None, :])
    vmem, dma = pltpu.VMEM, pltpu.SemaphoreType.DMA
    any_spec = pl.BlockSpec(memory_space=pl.ANY)
    vmem_spec = pl.BlockSpec(memory_space=vmem)
    return pl.pallas_call(
        kernel,
        out_shape=jax.ShapeDtypeStruct((TOK // 2, FEAT), BF16),
        in_specs=[any_spec] * 5 + [pl.BlockSpec(memory_space=pltpu.SMEM), vmem_spec, vmem_spec],
        out_specs=vmem_spec,
        scratch_shapes=[
            vmem((2, TOK // 2, FEAT), BF16),
            vmem((RING, TOK, DEPTH), BF16),
            vmem((RING * RING, TOK, DEPTH), BF16),
            vmem((HEADS, W_ROWS, HEAD), BF16),
            vmem((2, W_ROWS, 1024), BF16),
            vmem((2 * RING, W_ROWS, KV_COLS + Q_COLS), BF16),
            vmem((2 * RING, W_ROWS, KV_COLS + Q_COLS), BF16),
            vmem((2, 2 * HEAD, HALF), BF16),
            vmem((8, HEAD), jnp.int32),
            pltpu.SMEM((8, HEAD), jnp.int32),
            vmem((SPAN, HEAD), F32),
            vmem((SPAN, HEAD), F32),
            vmem((RING, SPAN, HEAD), BF16),
            vmem((RING, SPAN, HEAD), BF16),
            vmem((RING, RING, ROWS, 2 * HEAD), BF16),
            vmem((RING, RING, ROWS, 2 * HEAD), BF16),
            vmem((2, SPAN, HEAD), BF16),
            vmem((2, RING, ROWS, 2 * HEAD), BF16),
            vmem((RING, RING, RING, TOK, PART), BF16),
            vmem((RING, 2, 2, TOK, PART), BF16),
            vmem((RING, 2, RING, TOK, PART), BF16),
            vmem((RING, RING, TOK, PART), BF16),
            vmem((RING, RING, TOK, PART), BF16),
            vmem((RING, 2, TOK // 2, PART), BF16),
            vmem((2, RING, TOK // 2, PART), BF16),
            dma((6,)), dma((2,)), dma((2,)),
            dma((2 * RING,)), dma((2 * RING,)), dma((2 * RING,)), dma((2 * RING,)),
            dma((RING,)), dma((RING * RING,)), dma((RING * RING,)),
            dma((RING, RING)), dma((RING, RING)), dma((RING, RING)), dma((RING, RING)),
            dma((RING,)), dma((RING,)), dma((RING,)), dma((RING,)),
            dma((RING, 2)), dma((RING, 2)), dma((RING, 2)), dma((RING, 2)),
            dma((RING, RING)), dma((RING, RING)), dma((RING, 2)), dma((2, RING)),
        ],
        compiler_params=pltpu.CompilerParams(
            collective_id=0, has_side_effects=True, vmem_limit_bytes=56 << 20
        ),
        cost_estimate=pl.CostEstimate(flops=6 << 30, bytes_accessed=8 << 20, transcendentals=1 << 20),
    )(hidden_in, query_weight, key_weight, value_projection_weight, output_weight, head_order, positions, freq)


def solution(mesh):
    return jax.shard_map(
        shards,
        mesh=mesh,
        in_specs=(
            P(("replica", "tensor"), None),
            P("tensor", None),
            P("tensor", None),
            P("tensor", None),
            P("tensor", None),
            P(),
            P("replica"),
        ),
        out_specs=P(("replica", "tensor"), None),
        check_vma=False,
    )
```

```python
import math

import jax
import jax.numpy as jnp
import numpy as np
from jax import lax
from jax.experimental import pallas as pl
from jax.experimental.pallas import tpu as pltpu
from jax.sharding import PartitionSpec as P

MESH = pl.DeviceIdType.MESH
F32, BF16 = jnp.float32, jnp.bfloat16

HEAD = 128
RING = 4
TOK = 48
ROWS = RING * TOK
SPAN = RING * ROWS
FEAT = 4096
DEPTH = FEAT // RING
KV_COLS = RING * HEAD
Q_COLS = RING * 2 * HEAD
HALF = FEAT // 2
WIDE = HALF // 2
PART = HALF // RING
HEADS = 64
W_ROWS = 128
ROPE_BASE = 1000000.0
EXP_SCALE = math.log2(math.e) / math.sqrt(HEAD)


def kernel(
    x_hbm, wq_hbm, wk_hbm, wv_hbm, wo_hbm, order_ref, pos_ref, freq_ref,
    out_ref,
    xpair, xs, xall, wq, wkv, wsend, wall, wo2, inv_v, inv_s, cos_t, sin_t,
    ykv, ykv_in, yq, yq_in, kv, hbuf, obuf, f_in, o1_in, o1_sum, o2_in, fin_out, fin_in,
    loc_sem, d2d_s, d2d_r, w_s, w_r, e_s, z_s, z_r, x1_s, x2_s, x_r, ykv_s, ykv_r, yq_s, yq_r,
    kv_s, kv_r, h_s, h_r, f_s, f_r, o1_s, o1_r, o2_s, o2_r, fin_s, fin_r,
):
    t = lax.axis_index("tensor")
    z = lax.axis_index("replica")
    planes = lax.axis_size("replica")
    y, x, c = t // 8, (t // 2) % 4, t % 2
    first = c == 0
    p, s = jnp.where(first, x, y), jnp.where(first, y, x)
    oc = 1 - c
    part = z % 2
    beyond = {1: z + 1 < planes, -1: z > 0}

    def wrap(v):
        return lax.rem(v + 8, RING)

    def device(pp, ss):
        return jnp.where(first, 8 * ss + 2 * pp, 8 * pp + 2 * ss + 1)

    def slot(pp, ss):
        return jnp.where(first, RING * ss + pp, RING * pp + ss)

    def remote(src, dst, ss, rs, dev, dz=0):
        where = {"tensor": dev}
        if dz:
            where["replica"] = lax.rem(z + dz + planes, planes)
        return pltpu.make_async_remote_copy(
            src_ref=src, dst_ref=dst, send_sem=ss, recv_sem=rs,
            device_id=where, device_id_type=MESH,
        )

    partner = t + 1 - 2 * c

    barrier = pltpu.get_barrier_semaphore()

    def greet(dev, dz=0):
        where = {"tensor": dev}
        if dz:
            where["replica"] = lax.rem(z + dz + planes, planes)
        pl.semaphore_signal(barrier, inc=1, device_id=where, device_id_type=MESH)

    for d in range(1, RING):
        ring = device(wrap(p + d), s)
        greet(ring)
        greet(ring + 1 - 2 * c)
        greet(device(p, wrap(s + d)))
    greet(partner)
    for dz in (1, -1):

        @pl.when(beyond[dz])
        def _(dz=dz):
            greet(t, dz)


    @pl.when(first)
    def _():
        for d in range(1, RING):
            greet(8 * wrap(y + d) + 2 * x + 1)

    own_x = pltpu.make_async_copy(x_hbm, xpair.at[c], loc_sem.at[0])
    own_q = pltpu.make_async_copy(wq, wq, loc_sem.at[1])
    own_k = pltpu.make_async_copy(wk_hbm, wkv.at[0], loc_sem.at[2])
    own_v = pltpu.make_async_copy(wv_hbm, wkv.at[1], loc_sem.at[3])
    own_o = pltpu.make_async_copy(
        wo_hbm.at[:, pl.ds(pl.multiple_of(c * HALF, HALF), HALF)], wo2.at[c], loc_sem.at[4]
    )

    def load_head(i, _):
        cols = pl.ds(pl.multiple_of(i * HEAD, HEAD), HEAD)
        pltpu.make_async_copy(wq_hbm.at[:, cols], wq.at[i], loc_sem.at[1]).start()
        return 0

    own_k.start()
    own_v.start()
    lax.fori_loop(0, HEADS, load_head, 0, unroll=8)
    own_x.start()
    own_o.start()

    lane = lax.broadcasted_iota(jnp.int32, (8, HEAD), 1)

    def invert(i, acc):
        return jnp.where(lane == order_ref[i], i, acc)

    inv_v[...] = lax.fori_loop(0, HEADS, invert, jnp.zeros((8, HEAD), jnp.int32), unroll=8)
    to_scalars = pltpu.make_async_copy(inv_v, inv_s, loc_sem.at[5])
    to_scalars.start()

    ends = jnp.where(beyond[1], 0, 1) + jnp.where(beyond[-1], 0, 1)
    pl.semaphore_wait(barrier, 12 - ends + 3 * c)

    x_d2d = remote(x_hbm, xpair.at[c], d2d_s.at[0], d2d_r.at[0], partner)
    x_d2d.start()
    to_scalars.wait()
    own_k.wait()
    own_v.wait()
    own_q.wait()

    sends, extra, forwards = [], [], []
    half_rows = W_ROWS // 2
    moved = pl.ds(pl.multiple_of(part * half_rows, half_rows), half_rows)
    brought = pl.ds(pl.multiple_of((1 - part) * half_rows, half_rows), half_rows)

    def weights(other, d):
        cc = jnp.where(other == 1, oc, c)
        cc_first = cc == 0
        pcc = jnp.where(cc_first, x, y)
        pp = wrap(pcc + d)
        own = other == 0 and d == 0
        place = wall.at[2 * p + c] if own else wsend.at[RING * other + d]

        def fill(rows):
            def step(ss, _):
                tt = jnp.where(cc_first, 8 * ss + 2 * pp, 8 * pp + 2 * ss + 1)
                group = pl.multiple_of((tt // 4) * HEAD, HEAD)
                place[rows, pl.ds(pl.multiple_of(ss * HEAD, HEAD), HEAD)] = wkv[
                    cc, rows, pl.ds(group, HEAD)
                ]
                for i in range(2):
                    at = pl.multiple_of(KV_COLS + (2 * ss + i) * HEAD, HEAD)
                    place[rows, pl.ds(at, HEAD)] = wq[inv_s[0, 2 * tt + i], rows]
                return 0

            lax.fori_loop(0, RING, step, 0)

        def copy_of(rows, leave, arrive):
            dev = jnp.where(cc_first, 8 * y + 2 * pp, 8 * pp + 2 * x + 1)
            return remote(
                place.at[rows], wall.at[2 * pcc + c, rows],
                leave.at[RING * other + d], arrive.at[2 * pcc + c], dev,
            )

        rows = moved if d else pl.ds(0, W_ROWS)
        fill(rows)
        if own:
            return None
        copy = copy_of(rows, w_s, w_r)
        sends.append(copy)
        if d in (1, 3):
            alone = jnp.logical_not(beyond[1 if other else -1])
            extra.append((alone, fill, copy_of(brought, e_s, z_r)))
        return copy

    near = [weights(other, d) for d in (1, 3) for other in (0, 1)]
    for copy in near:
        copy.start()

    own_x.wait()
    remote(x_hbm, xpair.at[oc], d2d_s.at[0], d2d_r.at[0], partner).wait_recv()
    mine = slot(p, s)
    for d in (1, 3, 2, 0):
        ss = wrap(s + d)
        for pp in range(RING):
            feat = pl.multiple_of(
                jnp.where(first, DEPTH * ss + 256 * pp, DEPTH * pp + 256 * ss), 256
            )
            rows = jnp.concatenate(
                [xpair[0, :, pl.ds(feat, 256)].astype(F32), xpair[1, :, pl.ds(feat, 256)].astype(F32)],
                axis=0,
            ).astype(BF16)
            if d == 0:
                xall[mine, :, 256 * pp : 256 * pp + 256] = rows
            else:
                xs[d, :, 256 * pp : 256 * pp + 256] = rows
        if d:
            copy = remote(xs.at[d], xall.at[mine], x1_s.at[d], x_r.at[mine], device(p, ss))
            copy.start()
            sends.append(copy)

    far = [weights(other, 2) for other in (0, 1)]
    weights(1, 0).start()
    weights(0, 0)
    x_d2d.wait_send()
    wo_d2d = remote(
        wo_hbm.at[:, pl.ds(pl.multiple_of(oc * HALF, HALF), HALF)], wo2.at[c],
        d2d_s.at[1], d2d_r.at[1], partner,
    )
    wo_d2d.start()

    def arrived(m):
        remote(xall.at[m], xall.at[m], x1_s.at[0], x_r.at[m], partner).wait_recv()

    def from_plane(e):
        for other in (0, 1):
            k = 2 * wrap(p + e) + (oc if other else c)
            here = wall.at[k, moved]
            remote(here, here, w_s.at[0], w_r.at[k], partner).wait_recv()
            dz = -1 if other else 1
            copy = remote(here, here, z_s.at[k], z_r.at[k], t, dz)
            pl.when(beyond[dz])(copy.start)
            forwards.append((beyond[dz], copy))
            if e == 2:
                last = z == (planes - 2 if other else 1)
                copy = remote(here, here, e_s.at[RING * other + e], z_r.at[k], t, -dz)
                pl.when(last)(copy.start)
                forwards.append((last, copy))

    def forward(d):
        m = slot(p, wrap(s + d))
        if d:
            arrived(m)
        for e in (1, 3, 2):
            copy = remote(
                xall.at[m], xall.at[m], x2_s.at[RING * e + d], x_r.at[m], device(wrap(p + e), s)
            )
            copy.start()
            sends.append(copy)

    eye = lax.broadcasted_iota(jnp.int32, (HEAD, HEAD), 0) == lax.broadcasted_iota(
        jnp.int32, (HEAD, HEAD), 1
    )
    sign = jnp.where(lax.broadcasted_iota(jnp.int32, (HEAD, HEAD), 1) < HEAD // 2, -1.0, 1.0)

    def table(n, _):
        at = pl.ds(pl.multiple_of(n * HEAD, HEAD), HEAD)
        line = pos_ref[at].astype(F32)
        column = jnp.sum(jnp.where(eye, line[None, :], 0.0), axis=1, keepdims=True)
        ang = column * freq_ref[...]
        cos_t[at, :] = jnp.cos(ang)
        sin_t[at, :] = jnp.sin(ang) * sign
        return 0

    lax.fori_loop(0, SPAN // HEAD, table, 0)

    for copy in near:
        copy.wait_send()
        sends.remove(copy)
    for copy in far:
        copy.start()
    for alone, fill, copy in extra:

        @pl.when(alone)
        def _(fill=fill, copy=copy):
            fill(brought)
            copy.start()

    from_plane(1)
    from_plane(3)
    for d in range(RING):
        forward(d)
    from_plane(2)
    own_o.wait()
    wo_d2d.wait()
    k = 2 * p + oc
    remote(wall.at[k], wall.at[k], w_s.at[0], w_r.at[k], partner).wait_recv()
    for e in (1, 3, 2):
        for other in (0, 1):
            k = 2 * wrap(p + e) + (oc if other else c)
            there = wall.at[k, brought]
            remote(there, there, z_s.at[k], z_r.at[k], partner).wait_recv()
    for e in (1, 3, 2):
        for ss in range(RING):
            arrived(slot(wrap(p + e), ss))

    q_sends = []

    def partial(i):
        at = pl.ds(i * ROWS, ROWS)
        r = jnp.dot(
            xall[RING * i : RING * i + RING].reshape(ROWS, DEPTH),
            wall[...].reshape(DEPTH, KV_COLS + Q_COLS),
            preferred_element_type=F32,
        ).astype(BF16)
        for ss in range(RING):
            ykv[ss, at, :] = r[:, ss * HEAD : (ss + 1) * HEAD]
            yq[i, ss] = r[:, KV_COLS + ss * 2 * HEAD : KV_COLS + (ss + 1) * 2 * HEAD]

    def send_kv(i):
        at = pl.ds(i * ROWS, ROWS)
        for d in (2, 1, 3):
            ss = wrap(s + d)
            copy = remote(
                ykv.at[ss, at], ykv_in.at[s, at], ykv_s.at[i, d], ykv_r.at[i, s], device(p, ss)
            )
            copy.start()
            sends.append(copy)

    def send_q(i):
        group = []
        for d in (2, 1, 3):
            ss = wrap(s + d)
            copy = remote(yq.at[i, ss], yq_in.at[i, s], yq_s.at[i, d], yq_r.at[i, s], device(p, ss))
            copy.start()
            group.append(copy)
        q_sends.append(group)

    def sent_q(i):
        for copy in q_sends[i]:
            copy.wait_send()

    def gather_kv(i):
        at = pl.ds(i * ROWS, ROWS)
        total = ykv[s, at, :].astype(F32)
        for d in (1, 2, 3):
            ss = wrap(s + d)
            remote(
                ykv.at[ss, at], ykv_in.at[ss, at], ykv_s.at[i, d], ykv_r.at[i, ss], partner
            ).wait_recv()
            total += ykv_in[ss, at, :].astype(F32)
        whole = total.astype(BF16).astype(F32)
        turned = whole * cos_t[at, :] + pltpu.roll(whole, HEAD // 2, 1) * sin_t[at, :]
        kv[c, at, :] = jnp.where(first, turned, whole).astype(BF16)
        copy = remote(kv.at[c, at], kv.at[c, at], kv_s.at[i], kv_r.at[i], partner)
        copy.start()
        sends.append(copy)

    def attend(i):
        at = pl.ds(i * ROWS, ROWS)
        remote(kv.at[oc, at], kv.at[oc, at], kv_s.at[i], kv_r.at[i], partner).wait_recv()
        total = yq[i, s].astype(F32)
        for d in (1, 2, 3):
            ss = wrap(s + d)
            remote(yq.at[i, ss], yq_in.at[i, ss], yq_s.at[i, d], yq_r.at[i, ss], partner).wait_recv()
            total += yq_in[i, ss].astype(F32)
        keys = (i + 1) * ROWS
        row = i * ROWS + lax.broadcasted_iota(jnp.int32, (ROWS, keys), 0)
        seen = lax.broadcasted_iota(jnp.int32, (ROWS, keys), 1) <= row
        for h in range(2):
            v = total[:, h * HEAD : (h + 1) * HEAD]
            q = (v * cos_t[at, :] + pltpu.roll(v, HEAD // 2, 1) * sin_t[at, :]).astype(BF16)
            scores = lax.dot_general(
                q, kv[0, :keys, :], (((1,), (1,)), ((), ())), preferred_element_type=F32
            )
            scores = jnp.where(seen, scores, -jnp.inf)
            top = jnp.max(scores, axis=1, keepdims=True)
            expo = jnp.exp2((scores - top) * EXP_SCALE)
            norm = jnp.sum(expo, axis=1, keepdims=True)
            head = jnp.dot(expo.astype(BF16), kv[1, :keys, :], preferred_element_type=F32) / norm
            hbuf[c, i, :, h * HEAD : (h + 1) * HEAD] = head.astype(BF16)
        copy = remote(hbuf.at[c, i], hbuf.at[c, i], h_s.at[i], h_r.at[i], partner)
        copy.start()
        sends.append(copy)

    def project(i):
        remote(hbuf.at[oc, i], hbuf.at[oc, i], h_s.at[i], h_r.at[i], partner).wait_recv()
        far_place = wrap(p + 2)
        for w in range(2):
            cols = pl.ds(w * WIDE, WIDE)
            r = jnp.dot(hbuf[0, i], wo2[0, :, cols], preferred_element_type=F32)
            r += jnp.dot(hbuf[1, i], wo2[1, :, cols], preferred_element_type=F32)
            r = r.astype(BF16)
            for b in range(RING):
                for v in range(2):
                    g = 2 * w + v
                    obuf[i, jnp.where(first, b, g), jnp.where(first, g, b)] = r[
                        b * TOK : (b + 1) * TOK, v * PART : (v + 1) * PART
                    ]
        if i == RING - 1:
            for d, w in ((2, 2), (1, 0), (3, 1)):
                place = wrap(p + d)
                copy = remote(
                    obuf.at[i, place], o1_in.at[i, w], o1_s.at[i, w], o1_r.at[i, w], device(place, s)
                )
                copy.start()
                sends.append(copy)
            return
        for d, w in ((1, 0), (3, 1)):
            copy = remote(
                obuf.at[i, far_place, pl.ds(2 * w, 2)], f_in.at[i, w], f_s.at[i, w], f_r.at[i, w],
                device(wrap(p + d), s),
            )
            copy.start()
            sends.append(copy)

    def fold(i):
        for d, w in ((1, 0), (3, 1)):
            place, half = wrap(p + d), pl.ds(2 * w, 2)
            remote(f_in.at[i, w], f_in.at[i, w], f_s.at[i, w], f_r.at[i, w], partner).wait_recv()
            obuf[i, place, half] = (
                obuf[i, place, half].astype(F32) + f_in[i, w].astype(F32)
            ).astype(BF16)
            copy = remote(
                obuf.at[i, place], o1_in.at[i, w], o1_s.at[i, w], o1_r.at[i, w], device(place, s)
            )
            copy.start()
            sends.append(copy)

    def combine(i):
        total = obuf[i, p].astype(F32)
        for w in range(3 if i == RING - 1 else 2):
            remote(o1_in.at[i, w], o1_in.at[i, w], o1_s.at[i, w], o1_r.at[i, w], partner).wait_recv()
            total += o1_in[i, w].astype(F32)
        o1_sum[i] = total.astype(BF16)
        for d in (2, 1, 3):
            ss = wrap(s + d)
            copy = remote(
                o1_sum.at[i, ss], o2_in.at[i, s], o2_s.at[i, d], o2_r.at[i, s], device(p, ss)
            )
            copy.start()
            sends.append(copy)

    def final(i, core):
        return remote(
            fin_out.at[i, core], fin_in.at[c, y], fin_s.at[i, core], fin_r.at[c, y],
            8 * i + 2 * x + core,
        )

    def finish(i):
        total = o1_sum[i, s].astype(F32)
        for d in (1, 2, 3):
            ss = wrap(s + d)
            remote(o1_sum.at[i, 0], o2_in.at[i, ss], o2_s.at[i, d], o2_r.at[i, ss], partner).wait_recv()
            total += o2_in[i, ss].astype(F32)
        for core in range(2):
            rows = total[core * (TOK // 2) : (core + 1) * (TOK // 2)].astype(BF16)
            fin_out[i, core] = rows
            mine_now = jnp.logical_and(y == i, c == core)

            @pl.when(mine_now)
            def _(rows=rows):
                fin_in[c, y] = rows

            @pl.when(jnp.logical_not(mine_now))
            def _(core=core):
                final(i, core).start()

    partial(0)
    send_kv(0)
    send_q(0)
    partial(1)
    partial(2)
    partial(3)
    send_kv(1)
    send_q(1)
    send_kv(2)
    send_kv(3)
    gather_kv(0)
    sent_q(0)
    send_q(2)
    gather_kv(1)
    sent_q(1)
    send_q(3)
    attend(0)
    attend(1)
    project(0)
    gather_kv(2)
    project(1)
    gather_kv(3)
    fold(0)
    attend(2)
    fold(1)
    attend(3)
    project(2)
    combine(0)
    project(3)
    fold(2)
    combine(1)
    finish(0)
    combine(2)
    finish(1)
    combine(3)
    finish(2)
    finish(3)

    sent_q(2)
    sent_q(3)
    for copy in sends:
        copy.wait_send()
    for alone, _, copy in extra:
        pl.when(alone)(copy.wait_send)
    for active, copy in forwards:
        pl.when(active)(copy.wait_send)
    for i in range(RING):
        for core in range(2):

            @pl.when(jnp.logical_or(y != i, c != core))
            def _(i=i, core=core):
                final(i, core).wait_send()

    for cc in range(2):
        for yy in range(RING):

            @pl.when(jnp.logical_or(y != yy, c != cc))
            def _(cc=cc, yy=yy):
                remote(
                    fin_out.at[0, 0], fin_in.at[cc, yy], fin_s.at[0, 0], fin_r.at[cc, yy], partner
                ).wait_recv()

            col = cc * HALF + yy * PART
            out_ref[:, col : col + PART] = fin_in[cc, yy]


def shards(hidden_in, query_weight, key_weight, value_projection_weight, output_weight, head_order, positions):
    half = np.float32(ROPE_BASE) ** (
        np.float32(-2.0) * np.arange(HEAD // 2, dtype=np.float32) / np.float32(HEAD)
    )
    freq = jnp.asarray(np.concatenate([half, half])[None, :])
    vmem, dma = pltpu.VMEM, pltpu.SemaphoreType.DMA
    any_spec = pl.BlockSpec(memory_space=pl.ANY)
    vmem_spec = pl.BlockSpec(memory_space=vmem)
    return pl.pallas_call(
        kernel,
        out_shape=jax.ShapeDtypeStruct((TOK // 2, FEAT), BF16),
        in_specs=[any_spec] * 5 + [pl.BlockSpec(memory_space=pltpu.SMEM), vmem_spec, vmem_spec],
        out_specs=vmem_spec,
        scratch_shapes=[
            vmem((2, TOK // 2, FEAT), BF16),
            vmem((RING, TOK, DEPTH), BF16),
            vmem((RING * RING, TOK, DEPTH), BF16),
            vmem((HEADS, W_ROWS, HEAD), BF16),
            vmem((2, W_ROWS, 1024), BF16),
            vmem((2 * RING, W_ROWS, KV_COLS + Q_COLS), BF16),
            vmem((2 * RING, W_ROWS, KV_COLS + Q_COLS), BF16),
            vmem((2, 2 * HEAD, HALF), BF16),
            vmem((8, HEAD), jnp.int32),
            pltpu.SMEM((8, HEAD), jnp.int32),
            vmem((SPAN, HEAD), F32),
            vmem((SPAN, HEAD), F32),
            vmem((RING, SPAN, HEAD), BF16),
            vmem((RING, SPAN, HEAD), BF16),
            vmem((RING, RING, ROWS, 2 * HEAD), BF16),
            vmem((RING, RING, ROWS, 2 * HEAD), BF16),
            vmem((2, SPAN, HEAD), BF16),
            vmem((2, RING, ROWS, 2 * HEAD), BF16),
            vmem((RING, RING, RING, TOK, PART), BF16),
            vmem((RING, 2, 2, TOK, PART), BF16),
            vmem((RING, 3, RING, TOK, PART), BF16),
            vmem((RING, RING, TOK, PART), BF16),
            vmem((RING, RING, TOK, PART), BF16),
            vmem((RING, 2, TOK // 2, PART), BF16),
            vmem((2, RING, TOK // 2, PART), BF16),
            dma((6,)), dma((2,)), dma((2,)),
            dma((2 * RING,)), dma((2 * RING,)), dma((2 * RING,)), dma((2 * RING,)), dma((2 * RING,)),
            dma((RING,)), dma((RING * RING,)), dma((RING * RING,)),
            dma((RING, RING)), dma((RING, RING)), dma((RING, RING)), dma((RING, RING)),
            dma((RING,)), dma((RING,)), dma((RING,)), dma((RING,)),
            dma((RING, 2)), dma((RING, 2)), dma((RING, 3)), dma((RING, 3)),
            dma((RING, RING)), dma((RING, RING)), dma((RING, 2)), dma((2, RING)),
        ],
        compiler_params=pltpu.CompilerParams(
            collective_id=0, has_side_effects=True, vmem_limit_bytes=56 << 20
        ),
        cost_estimate=pl.CostEstimate(flops=6 << 30, bytes_accessed=8 << 20, transcendentals=1 << 20),
    )(hidden_in, query_weight, key_weight, value_projection_weight, output_weight, head_order, positions, freq)


def solution(mesh):
    return jax.shard_map(
        shards,
        mesh=mesh,
        in_specs=(
            P(("replica", "tensor"), None),
            P("tensor", None),
            P("tensor", None),
            P("tensor", None),
            P("tensor", None),
            P(),
            P("replica"),
        ),
        out_specs=P(("replica", "tensor"), None),
        check_vma=False,
    )
```

```python
import math

import jax
import jax.numpy as jnp
import numpy as np
from jax import lax
from jax.experimental import pallas as pl
from jax.experimental.pallas import tpu as pltpu
from jax.sharding import PartitionSpec as P

MESH = pl.DeviceIdType.MESH
F32, BF16 = jnp.float32, jnp.bfloat16

HEAD = 128
RING = 4
TOK = 48
ROWS = RING * TOK
SPAN = RING * ROWS
FEAT = 4096
DEPTH = FEAT // RING
KV_COLS = RING * HEAD
Q_COLS = RING * 2 * HEAD
HALF = FEAT // 2
WIDE = HALF // 2
PART = HALF // RING
HEADS = 64
W_ROWS = 128
ROPE_BASE = 1000000.0
EXP_SCALE = math.log2(math.e) / math.sqrt(HEAD)


def kernel(
    x_hbm, wq_hbm, wk_hbm, wv_hbm, wo_hbm, order_ref, pos_ref, freq_ref,
    out_ref,
    xpair, xs, xall, wq, wkv, wsend, wall, wo2, inv_v, inv_s, cos_t, sin_t,
    ykv, ykv_in, yq, yq_in, kv, hbuf, obuf, f_in, o1_in, o1_sum, o2_in, fin_out, fin_in,
    loc_sem, d2d_s, d2d_r, w_s, w_r, e_s, z_s, z_r, x1_s, x2_s, x_r, ykv_s, ykv_r, yq_s, yq_r,
    kv_s, kv_r, h_s, h_r, f_s, f_r, o1_s, o1_r, o2_s, o2_r, fin_s, fin_r,
):
    t = lax.axis_index("tensor")
    z = lax.axis_index("replica")
    planes = lax.axis_size("replica")
    y, x, c = t // 8, (t // 2) % 4, t % 2
    first = c == 0
    p, s = jnp.where(first, x, y), jnp.where(first, y, x)
    oc = 1 - c
    part = z % 2
    beyond = {1: z + 1 < planes, -1: z > 0}

    def wrap(v):
        return lax.rem(v + 8, RING)

    def device(pp, ss):
        return jnp.where(first, 8 * ss + 2 * pp, 8 * pp + 2 * ss + 1)

    def slot(pp, ss):
        return jnp.where(first, RING * ss + pp, RING * pp + ss)

    def remote(src, dst, ss, rs, dev, dz=0):
        where = {"tensor": dev}
        if dz:
            where["replica"] = lax.rem(z + dz + planes, planes)
        return pltpu.make_async_remote_copy(
            src_ref=src, dst_ref=dst, send_sem=ss, recv_sem=rs,
            device_id=where, device_id_type=MESH,
        )

    partner = t + 1 - 2 * c

    barrier = pltpu.get_barrier_semaphore()

    def greet(dev, dz=0):
        where = {"tensor": dev}
        if dz:
            where["replica"] = lax.rem(z + dz + planes, planes)
        pl.semaphore_signal(barrier, inc=1, device_id=where, device_id_type=MESH)

    for d in range(1, RING):
        ring = device(wrap(p + d), s)
        greet(ring)
        greet(ring + 1 - 2 * c)
        greet(device(p, wrap(s + d)))
    greet(partner)
    for dz in (1, -1):

        @pl.when(beyond[dz])
        def _(dz=dz):
            greet(t, dz)


    @pl.when(first)
    def _():
        for d in range(1, RING):
            greet(8 * wrap(y + d) + 2 * x + 1)

    own_x = pltpu.make_async_copy(x_hbm, xpair.at[c], loc_sem.at[0])
    own_q = pltpu.make_async_copy(wq, wq, loc_sem.at[1])
    own_k = pltpu.make_async_copy(wk_hbm, wkv.at[0], loc_sem.at[2])
    own_v = pltpu.make_async_copy(wv_hbm, wkv.at[1], loc_sem.at[3])
    own_o = pltpu.make_async_copy(
        wo_hbm.at[:, pl.ds(pl.multiple_of(c * HALF, HALF), HALF)], wo2.at[c], loc_sem.at[4]
    )

    def load_head(i, _):
        cols = pl.ds(pl.multiple_of(i * HEAD, HEAD), HEAD)
        pltpu.make_async_copy(wq_hbm.at[:, cols], wq.at[i], loc_sem.at[1]).start()
        return 0

    own_k.start()
    own_v.start()
    lax.fori_loop(0, HEADS, load_head, 0, unroll=8)
    own_x.start()
    own_o.start()

    lane = lax.broadcasted_iota(jnp.int32, (8, HEAD), 1)

    def invert(i, acc):
        return jnp.where(lane == order_ref[i], i, acc)

    inv_v[...] = lax.fori_loop(0, HEADS, invert, jnp.zeros((8, HEAD), jnp.int32), unroll=8)
    to_scalars = pltpu.make_async_copy(inv_v, inv_s, loc_sem.at[5])
    to_scalars.start()

    ends = jnp.where(beyond[1], 0, 1) + jnp.where(beyond[-1], 0, 1)
    pl.semaphore_wait(barrier, 12 - ends + 3 * c)

    x_d2d = remote(x_hbm, xpair.at[c], d2d_s.at[0], d2d_r.at[0], partner)
    x_d2d.start()
    to_scalars.wait()
    own_k.wait()
    own_v.wait()
    own_q.wait()

    sends, extra, forwards = [], [], []
    half_rows = W_ROWS // 2
    moved = pl.ds(pl.multiple_of(part * half_rows, half_rows), half_rows)
    brought = pl.ds(pl.multiple_of((1 - part) * half_rows, half_rows), half_rows)

    def weights(other, d):
        cc = jnp.where(other == 1, oc, c)
        cc_first = cc == 0
        pcc = jnp.where(cc_first, x, y)
        pp = wrap(pcc + d)
        own = other == 0 and d == 0
        place = wall.at[2 * p + c] if own else wsend.at[RING * other + d]

        def fill(rows):
            def step(ss, _):
                tt = jnp.where(cc_first, 8 * ss + 2 * pp, 8 * pp + 2 * ss + 1)
                group = pl.multiple_of((tt // 4) * HEAD, HEAD)
                place[rows, pl.ds(pl.multiple_of(ss * HEAD, HEAD), HEAD)] = wkv[
                    cc, rows, pl.ds(group, HEAD)
                ]
                for i in range(2):
                    at = pl.multiple_of(KV_COLS + (2 * ss + i) * HEAD, HEAD)
                    place[rows, pl.ds(at, HEAD)] = wq[inv_s[0, 2 * tt + i], rows]
                return 0

            lax.fori_loop(0, RING, step, 0)

        def copy_of(rows, leave, arrive):
            dev = jnp.where(cc_first, 8 * y + 2 * pp, 8 * pp + 2 * x + 1)
            return remote(
                place.at[rows], wall.at[2 * pcc + c, rows],
                leave.at[RING * other + d], arrive.at[2 * pcc + c], dev,
            )

        rows = moved if d else pl.ds(0, W_ROWS)
        fill(rows)
        if own:
            return None
        copy = copy_of(rows, w_s, w_r)
        sends.append(copy)
        if d in (1, 3):
            alone = jnp.logical_not(beyond[1 if other else -1])
            extra.append((alone, fill, copy_of(brought, e_s, z_r)))
        return copy

    near = [weights(other, d) for d in (1, 3) for other in (0, 1)]
    for copy in near:
        copy.start()

    own_x.wait()
    remote(x_hbm, xpair.at[oc], d2d_s.at[0], d2d_r.at[0], partner).wait_recv()
    mine = slot(p, s)
    for d in (1, 3, 2, 0):
        ss = wrap(s + d)
        for pp in range(RING):
            feat = pl.multiple_of(
                jnp.where(first, DEPTH * ss + 256 * pp, DEPTH * pp + 256 * ss), 256
            )
            rows = jnp.concatenate(
                [xpair[0, :, pl.ds(feat, 256)].astype(F32), xpair[1, :, pl.ds(feat, 256)].astype(F32)],
                axis=0,
            ).astype(BF16)
            if d == 0:
                xall[mine, :, 256 * pp : 256 * pp + 256] = rows
            else:
                xs[d, :, 256 * pp : 256 * pp + 256] = rows
        if d:
            copy = remote(xs.at[d], xall.at[mine], x1_s.at[d], x_r.at[mine], device(p, ss))
            copy.start()
            sends.append(copy)

    far = [weights(other, 2) for other in (0, 1)]
    weights(1, 0).start()
    weights(0, 0)
    x_d2d.wait_send()
    wo_d2d = remote(
        wo_hbm.at[:, pl.ds(pl.multiple_of(oc * HALF, HALF), HALF)], wo2.at[c],
        d2d_s.at[1], d2d_r.at[1], partner,
    )
    wo_d2d.start()

    def arrived(m):
        remote(xall.at[m], xall.at[m], x1_s.at[0], x_r.at[m], partner).wait_recv()

    def from_plane(e):
        for other in (0, 1):
            k = 2 * wrap(p + e) + (oc if other else c)
            here = wall.at[k, moved]
            remote(here, here, w_s.at[0], w_r.at[k], partner).wait_recv()
            dz = -1 if other else 1
            copy = remote(here, here, z_s.at[k], z_r.at[k], t, dz)
            pl.when(beyond[dz])(copy.start)
            forwards.append((beyond[dz], copy))
            if e == 2:
                last = z == (planes - 2 if other else 1)
                copy = remote(here, here, e_s.at[RING * other + e], z_r.at[k], t, -dz)
                pl.when(last)(copy.start)
                forwards.append((last, copy))

    def forward(d):
        m = slot(p, wrap(s + d))
        if d:
            arrived(m)
        for e in (1, 3, 2):
            copy = remote(
                xall.at[m], xall.at[m], x2_s.at[RING * e + d], x_r.at[m], device(wrap(p + e), s)
            )
            copy.start()
            sends.append(copy)

    eye = lax.broadcasted_iota(jnp.int32, (HEAD, HEAD), 0) == lax.broadcasted_iota(
        jnp.int32, (HEAD, HEAD), 1
    )
    sign = jnp.where(lax.broadcasted_iota(jnp.int32, (HEAD, HEAD), 1) < HEAD // 2, -1.0, 1.0)

    def table(n, _):
        at = pl.ds(pl.multiple_of(n * HEAD, HEAD), HEAD)
        line = pos_ref[at].astype(F32)
        column = jnp.sum(jnp.where(eye, line[None, :], 0.0), axis=1, keepdims=True)
        ang = column * freq_ref[...]
        cos_t[at, :] = jnp.cos(ang)
        sin_t[at, :] = jnp.sin(ang) * sign
        return 0

    lax.fori_loop(0, SPAN // HEAD, table, 0)

    for copy in near:
        copy.wait_send()
        sends.remove(copy)
    for copy in far:
        copy.start()
    for alone, fill, copy in extra:

        @pl.when(alone)
        def _(fill=fill, copy=copy):
            fill(brought)
            copy.start()

    from_plane(1)
    from_plane(3)
    for d in range(RING):
        forward(d)
    from_plane(2)
    own_o.wait()
    wo_d2d.wait()
    k = 2 * p + oc
    remote(wall.at[k], wall.at[k], w_s.at[0], w_r.at[k], partner).wait_recv()
    for e in (1, 3, 2):
        for other in (0, 1):
            k = 2 * wrap(p + e) + (oc if other else c)
            there = wall.at[k, brought]
            remote(there, there, z_s.at[k], z_r.at[k], partner).wait_recv()
    for e in (1, 3, 2):
        for ss in range(RING):
            arrived(slot(wrap(p + e), ss))

    q_sends = []

    def partial(i):
        at = pl.ds(i * ROWS, ROWS)
        r = jnp.dot(
            xall[RING * i : RING * i + RING].reshape(ROWS, DEPTH),
            wall[...].reshape(DEPTH, KV_COLS + Q_COLS),
            preferred_element_type=F32,
        ).astype(BF16)
        for ss in range(RING):
            ykv[ss, at, :] = r[:, ss * HEAD : (ss + 1) * HEAD]
            yq[i, ss] = r[:, KV_COLS + ss * 2 * HEAD : KV_COLS + (ss + 1) * 2 * HEAD]

    def send_kv(i):
        at = pl.ds(i * ROWS, ROWS)
        for d in (2, 1, 3):
            ss = wrap(s + d)
            copy = remote(
                ykv.at[ss, at], ykv_in.at[s, at], ykv_s.at[i, d], ykv_r.at[i, s], device(p, ss)
            )
            copy.start()
            sends.append(copy)

    def send_q(i):
        group = []
        for d in (2, 1, 3):
            ss = wrap(s + d)
            copy = remote(yq.at[i, ss], yq_in.at[i, s], yq_s.at[i, d], yq_r.at[i, s], device(p, ss))
            copy.start()
            group.append(copy)
        q_sends.append(group)

    def sent_q(i):
        for copy in q_sends[i]:
            copy.wait_send()

    def gather_kv(i):
        at = pl.ds(i * ROWS, ROWS)
        total = ykv[s, at, :].astype(F32)
        for d in (1, 2, 3):
            ss = wrap(s + d)
            remote(
                ykv.at[ss, at], ykv_in.at[ss, at], ykv_s.at[i, d], ykv_r.at[i, ss], partner
            ).wait_recv()
            total += ykv_in[ss, at, :].astype(F32)
        whole = total.astype(BF16).astype(F32)
        turned = whole * cos_t[at, :] + pltpu.roll(whole, HEAD // 2, 1) * sin_t[at, :]
        kv[c, at, :] = jnp.where(first, turned, whole).astype(BF16)
        copy = remote(kv.at[c, at], kv.at[c, at], kv_s.at[i], kv_r.at[i], partner)
        copy.start()
        sends.append(copy)

    def attend(i):
        at = pl.ds(i * ROWS, ROWS)
        remote(kv.at[oc, at], kv.at[oc, at], kv_s.at[i], kv_r.at[i], partner).wait_recv()
        total = yq[i, s].astype(F32)
        for d in (1, 2, 3):
            ss = wrap(s + d)
            remote(yq.at[i, ss], yq_in.at[i, ss], yq_s.at[i, d], yq_r.at[i, ss], partner).wait_recv()
            total += yq_in[i, ss].astype(F32)
        keys = (i + 1) * ROWS
        row = i * ROWS + lax.broadcasted_iota(jnp.int32, (ROWS, keys), 0)
        seen = lax.broadcasted_iota(jnp.int32, (ROWS, keys), 1) <= row
        for h in range(2):
            v = total[:, h * HEAD : (h + 1) * HEAD]
            q = (v * cos_t[at, :] + pltpu.roll(v, HEAD // 2, 1) * sin_t[at, :]).astype(BF16)
            scores = lax.dot_general(
                q, kv[0, :keys, :], (((1,), (1,)), ((), ())), preferred_element_type=F32
            )
            scores = jnp.where(seen, scores, -jnp.inf)
            top = jnp.max(scores, axis=1, keepdims=True)
            expo = jnp.exp2((scores - top) * EXP_SCALE)
            norm = jnp.sum(expo, axis=1, keepdims=True)
            head = jnp.dot(expo.astype(BF16), kv[1, :keys, :], preferred_element_type=F32) / norm
            hbuf[c, i, :, h * HEAD : (h + 1) * HEAD] = head.astype(BF16)
        copy = remote(hbuf.at[c, i], hbuf.at[c, i], h_s.at[i], h_r.at[i], partner)
        copy.start()
        sends.append(copy)

    def project(i):
        remote(hbuf.at[oc, i], hbuf.at[oc, i], h_s.at[i], h_r.at[i], partner).wait_recv()
        far_place = wrap(p + 2)
        for w in range(2):
            cols = pl.ds(w * WIDE, WIDE)
            r = jnp.dot(hbuf[0, i], wo2[0, :, cols], preferred_element_type=F32)
            r += jnp.dot(hbuf[1, i], wo2[1, :, cols], preferred_element_type=F32)
            r = r.astype(BF16)
            for b in range(RING):
                for v in range(2):
                    g = 2 * w + v
                    obuf[i, jnp.where(first, b, g), jnp.where(first, g, b)] = r[
                        b * TOK : (b + 1) * TOK, v * PART : (v + 1) * PART
                    ]
        if i == RING - 1:
            for d, w in ((2, 2), (1, 0), (3, 1)):
                place = wrap(p + d)
                copy = remote(
                    obuf.at[i, place], o1_in.at[i, w], o1_s.at[i, w], o1_r.at[i, w], device(place, s)
                )
                copy.start()
                sends.append(copy)
            return
        for d, w in ((1, 0), (3, 1)):
            copy = remote(
                obuf.at[i, far_place, pl.ds(2 * w, 2)], f_in.at[i, w], f_s.at[i, w], f_r.at[i, w],
                device(wrap(p + d), s),
            )
            copy.start()
            sends.append(copy)

    def fold(i):
        for d, w in ((1, 0), (3, 1)):
            place, half = wrap(p + d), pl.ds(2 * w, 2)
            remote(f_in.at[i, w], f_in.at[i, w], f_s.at[i, w], f_r.at[i, w], partner).wait_recv()
            obuf[i, place, half] = (
                obuf[i, place, half].astype(F32) + f_in[i, w].astype(F32)
            ).astype(BF16)
            copy = remote(
                obuf.at[i, place], o1_in.at[i, w], o1_s.at[i, w], o1_r.at[i, w], device(place, s)
            )
            copy.start()
            sends.append(copy)

    def combine(i):
        total = obuf[i, p].astype(F32)
        for w in range(3 if i == RING - 1 else 2):
            remote(o1_in.at[i, w], o1_in.at[i, w], o1_s.at[i, w], o1_r.at[i, w], partner).wait_recv()
            total += o1_in[i, w].astype(F32)
        o1_sum[i] = total.astype(BF16)
        for d in (2, 1, 3):
            ss = wrap(s + d)
            copy = remote(
                o1_sum.at[i, ss], o2_in.at[i, s], o2_s.at[i, d], o2_r.at[i, s], device(p, ss)
            )
            copy.start()
            sends.append(copy)

    def final(i, core):
        return remote(
            fin_out.at[i, core], fin_in.at[c, y], fin_s.at[i, core], fin_r.at[c, y],
            8 * i + 2 * x + core,
        )

    def finish(i):
        total = o1_sum[i, s].astype(F32)
        for d in (1, 2, 3):
            ss = wrap(s + d)
            remote(o1_sum.at[i, 0], o2_in.at[i, ss], o2_s.at[i, d], o2_r.at[i, ss], partner).wait_recv()
            total += o2_in[i, ss].astype(F32)
        for core in range(2):
            rows = total[core * (TOK // 2) : (core + 1) * (TOK // 2)].astype(BF16)
            fin_out[i, core] = rows
            mine_now = jnp.logical_and(y == i, c == core)

            @pl.when(mine_now)
            def _(rows=rows):
                fin_in[c, y] = rows

            @pl.when(jnp.logical_not(mine_now))
            def _(core=core):
                final(i, core).start()

    partial(0)
    send_kv(0)
    send_q(0)
    partial(1)
    partial(2)
    partial(3)
    send_kv(1)
    send_q(1)
    send_kv(2)
    send_kv(3)
    gather_kv(0)
    sent_q(0)
    send_q(2)
    gather_kv(1)
    sent_q(1)
    send_q(3)
    attend(0)
    attend(1)
    project(0)
    gather_kv(2)
    project(1)
    gather_kv(3)
    fold(0)
    attend(2)
    fold(1)
    attend(3)
    project(2)
    combine(0)
    project(3)
    fold(2)
    combine(1)
    finish(0)
    combine(2)
    finish(1)
    combine(3)
    finish(2)
    finish(3)

    sent_q(2)
    sent_q(3)
    for copy in sends:
        copy.wait_send()
    for alone, _, copy in extra:
        pl.when(alone)(copy.wait_send)
    for active, copy in forwards:
        pl.when(active)(copy.wait_send)
    for i in range(RING):
        for core in range(2):

            @pl.when(jnp.logical_or(y != i, c != core))
            def _(i=i, core=core):
                final(i, core).wait_send()

    for cc in range(2):
        for yy in range(RING):

            @pl.when(jnp.logical_or(y != yy, c != cc))
            def _(cc=cc, yy=yy):
                remote(
                    fin_out.at[0, 0], fin_in.at[cc, yy], fin_s.at[0, 0], fin_r.at[cc, yy], partner
                ).wait_recv()

            col = cc * HALF + yy * PART
            out_ref[:, col : col + PART] = fin_in[cc, yy]


def shards(hidden_in, query_weight, key_weight, value_projection_weight, output_weight, head_order, positions):
    half = np.float32(ROPE_BASE) ** (
        np.float32(-2.0) * np.arange(HEAD // 2, dtype=np.float32) / np.float32(HEAD)
    )
    freq = jnp.asarray(np.concatenate([half, half])[None, :])
    vmem, dma = pltpu.VMEM, pltpu.SemaphoreType.DMA
    any_spec = pl.BlockSpec(memory_space=pl.ANY)
    vmem_spec = pl.BlockSpec(memory_space=vmem)
    return pl.pallas_call(
        kernel,
        out_shape=pltpu.VMEM((TOK // 2, FEAT), BF16),
        in_specs=[any_spec] * 5 + [pl.BlockSpec(memory_space=pltpu.SMEM), vmem_spec, vmem_spec],
        out_specs=vmem_spec,
        scratch_shapes=[
            vmem((2, TOK // 2, FEAT), BF16),
            vmem((RING, TOK, DEPTH), BF16),
            vmem((RING * RING, TOK, DEPTH), BF16),
            vmem((HEADS, W_ROWS, HEAD), BF16),
            vmem((2, W_ROWS, 1024), BF16),
            vmem((2 * RING, W_ROWS, KV_COLS + Q_COLS), BF16),
            vmem((2 * RING, W_ROWS, KV_COLS + Q_COLS), BF16),
            vmem((2, 2 * HEAD, HALF), BF16),
            vmem((8, HEAD), jnp.int32),
            pltpu.SMEM((8, HEAD), jnp.int32),
            vmem((SPAN, HEAD), F32),
            vmem((SPAN, HEAD), F32),
            vmem((RING, SPAN, HEAD), BF16),
            vmem((RING, SPAN, HEAD), BF16),
            vmem((RING, RING, ROWS, 2 * HEAD), BF16),
            vmem((RING, RING, ROWS, 2 * HEAD), BF16),
            vmem((2, SPAN, HEAD), BF16),
            vmem((2, RING, ROWS, 2 * HEAD), BF16),
            vmem((RING, RING, RING, TOK, PART), BF16),
            vmem((RING, 2, 2, TOK, PART), BF16),
            vmem((RING, 3, RING, TOK, PART), BF16),
            vmem((RING, RING, TOK, PART), BF16),
            vmem((RING, RING, TOK, PART), BF16),
            vmem((RING, 2, TOK // 2, PART), BF16),
            vmem((2, RING, TOK // 2, PART), BF16),
            dma((6,)), dma((2,)), dma((2,)),
            dma((2 * RING,)), dma((2 * RING,)), dma((2 * RING,)), dma((2 * RING,)), dma((2 * RING,)),
            dma((RING,)), dma((RING * RING,)), dma((RING * RING,)),
            dma((RING, RING)), dma((RING, RING)), dma((RING, RING)), dma((RING, RING)),
            dma((RING,)), dma((RING,)), dma((RING,)), dma((RING,)),
            dma((RING, 2)), dma((RING, 2)), dma((RING, 3)), dma((RING, 3)),
            dma((RING, RING)), dma((RING, RING)), dma((RING, 2)), dma((2, RING)),
        ],
        compiler_params=pltpu.CompilerParams(
            collective_id=0, has_side_effects=True, vmem_limit_bytes=56 << 20
        ),
        cost_estimate=pl.CostEstimate(flops=6 << 30, bytes_accessed=8 << 20, transcendentals=1 << 20),
    )(hidden_in, query_weight, key_weight, value_projection_weight, output_weight, head_order, positions, freq)


def solution(mesh):
    return jax.shard_map(
        shards,
        mesh=mesh,
        in_specs=(
            P(("replica", "tensor"), None),
            P("tensor", None),
            P("tensor", None),
            P("tensor", None),
            P("tensor", None),
            P(),
            P("replica"),
        ),
        out_specs=P(("replica", "tensor"), None),
        check_vma=False,
    )
```

```python
import math

import jax
import jax.numpy as jnp
import numpy as np
from jax import lax
from jax.experimental import pallas as pl
from jax.experimental.pallas import tpu as pltpu
from jax.sharding import PartitionSpec as P

MESH = pl.DeviceIdType.MESH
F32, BF16 = jnp.float32, jnp.bfloat16

HEAD = 128
RING = 4
TOK = 48
ROWS = RING * TOK
SPAN = RING * ROWS
FEAT = 4096
DEPTH = FEAT // RING
KV_COLS = RING * HEAD
Q_COLS = RING * 2 * HEAD
HALF = FEAT // 2
WIDE = HALF // 2
PART = HALF // RING
HEADS = 64
W_ROWS = 128
ROPE_BASE = 1000000.0
EXP_SCALE = math.log2(math.e) / math.sqrt(HEAD)


def kernel(
    x_hbm, wq_hbm, wk_hbm, wv_hbm, wo_hbm, order_ref, pos_hbm, freq_hbm,
    out_ref,
    xpair, xs, xall, wq, wkv, wsend, wall, wo2, inv_v, inv_s, cos_t, sin_t,
    ykv, ykv_in, yq, yq_in, kv, hbuf, obuf, f_in, o1_in, o1_sum, o2_in, fin_out, fin_in,
    pos_ref, freq_ref, loc_sem, d2d_s, d2d_r, w_s, w_r, e_s, z_s, z_r, x1_s, x2_s, x_r, ykv_s, ykv_r, yq_s, yq_r,
    kv_s, kv_r, h_s, h_r, f_s, f_r, o1_s, o1_r, o2_s, o2_r, fin_s, fin_r,
):
    t = lax.axis_index("tensor")
    z = lax.axis_index("replica")
    planes = lax.axis_size("replica")
    y, x, c = t // 8, (t // 2) % 4, t % 2
    first = c == 0
    p, s = jnp.where(first, x, y), jnp.where(first, y, x)
    oc = 1 - c
    part = z % 2
    beyond = {1: z + 1 < planes, -1: z > 0}

    def wrap(v):
        return lax.rem(v + 8, RING)

    def device(pp, ss):
        return jnp.where(first, 8 * ss + 2 * pp, 8 * pp + 2 * ss + 1)

    def slot(pp, ss):
        return jnp.where(first, RING * ss + pp, RING * pp + ss)

    def remote(src, dst, ss, rs, dev, dz=0):
        where = {"tensor": dev}
        if dz:
            where["replica"] = lax.rem(z + dz + planes, planes)
        return pltpu.make_async_remote_copy(
            src_ref=src, dst_ref=dst, send_sem=ss, recv_sem=rs,
            device_id=where, device_id_type=MESH,
        )

    partner = t + 1 - 2 * c

    barrier = pltpu.get_barrier_semaphore()

    def greet(dev, dz=0):
        where = {"tensor": dev}
        if dz:
            where["replica"] = lax.rem(z + dz + planes, planes)
        pl.semaphore_signal(barrier, inc=1, device_id=where, device_id_type=MESH)

    for d in range(1, RING):
        ring = device(wrap(p + d), s)
        greet(ring)
        greet(ring + 1 - 2 * c)
        greet(device(p, wrap(s + d)))
    greet(partner)
    for dz in (1, -1):

        @pl.when(beyond[dz])
        def _(dz=dz):
            greet(t, dz)


    @pl.when(first)
    def _():
        for d in range(1, RING):
            greet(8 * wrap(y + d) + 2 * x + 1)

    own_x = pltpu.make_async_copy(x_hbm, xpair.at[c], loc_sem.at[0])
    own_q = pltpu.make_async_copy(wq, wq, loc_sem.at[1])
    own_k = pltpu.make_async_copy(wk_hbm, wkv.at[0], loc_sem.at[2])
    own_v = pltpu.make_async_copy(wv_hbm, wkv.at[1], loc_sem.at[3])
    own_o = pltpu.make_async_copy(
        wo_hbm.at[:, pl.ds(pl.multiple_of(c * HALF, HALF), HALF)], wo2.at[c], loc_sem.at[4]
    )

    def load_head(i, _):
        cols = pl.ds(pl.multiple_of(i * HEAD, HEAD), HEAD)
        pltpu.make_async_copy(wq_hbm.at[:, cols], wq.at[i], loc_sem.at[1]).start()
        return 0

    own_k.start()
    own_v.start()
    lax.fori_loop(0, HEADS, load_head, 0, unroll=8)
    own_x.start()
    own_o.start()
    own_pos = pltpu.make_async_copy(pos_hbm, pos_ref, loc_sem.at[6])
    own_freq = pltpu.make_async_copy(freq_hbm, freq_ref, loc_sem.at[7])
    own_pos.start()
    own_freq.start()

    lane = lax.broadcasted_iota(jnp.int32, (8, HEAD), 1)

    def invert(i, acc):
        return jnp.where(lane == order_ref[i], i, acc)

    inv_v[...] = lax.fori_loop(0, HEADS, invert, jnp.zeros((8, HEAD), jnp.int32), unroll=8)
    to_scalars = pltpu.make_async_copy(inv_v, inv_s, loc_sem.at[5])
    to_scalars.start()

    ends = jnp.where(beyond[1], 0, 1) + jnp.where(beyond[-1], 0, 1)
    pl.semaphore_wait(barrier, 12 - ends + 3 * c)

    x_d2d = remote(x_hbm, xpair.at[c], d2d_s.at[0], d2d_r.at[0], partner)
    x_d2d.start()
    to_scalars.wait()
    own_k.wait()
    own_v.wait()
    own_q.wait()

    sends, extra, forwards = [], [], []
    half_rows = W_ROWS // 2
    moved = pl.ds(pl.multiple_of(part * half_rows, half_rows), half_rows)
    brought = pl.ds(pl.multiple_of((1 - part) * half_rows, half_rows), half_rows)

    def weights(other, d):
        cc = jnp.where(other == 1, oc, c)
        cc_first = cc == 0
        pcc = jnp.where(cc_first, x, y)
        pp = wrap(pcc + d)
        own = other == 0 and d == 0
        place = wall.at[2 * p + c] if own else wsend.at[RING * other + d]

        def fill(rows):
            def step(ss, _):
                tt = jnp.where(cc_first, 8 * ss + 2 * pp, 8 * pp + 2 * ss + 1)
                group = pl.multiple_of((tt // 4) * HEAD, HEAD)
                place[rows, pl.ds(pl.multiple_of(ss * HEAD, HEAD), HEAD)] = wkv[
                    cc, rows, pl.ds(group, HEAD)
                ]
                for i in range(2):
                    at = pl.multiple_of(KV_COLS + (2 * ss + i) * HEAD, HEAD)
                    place[rows, pl.ds(at, HEAD)] = wq[inv_s[0, 2 * tt + i], rows]
                return 0

            lax.fori_loop(0, RING, step, 0)

        def copy_of(rows, leave, arrive):
            dev = jnp.where(cc_first, 8 * y + 2 * pp, 8 * pp + 2 * x + 1)
            return remote(
                place.at[rows], wall.at[2 * pcc + c, rows],
                leave.at[RING * other + d], arrive.at[2 * pcc + c], dev,
            )

        rows = moved if d else pl.ds(0, W_ROWS)
        fill(rows)
        if own:
            return None
        copy = copy_of(rows, w_s, w_r)
        sends.append(copy)
        if d in (1, 3):
            alone = jnp.logical_not(beyond[1 if other else -1])
            extra.append((alone, fill, copy_of(brought, e_s, z_r)))
        return copy

    near = [weights(other, d) for d in (1, 3) for other in (0, 1)]
    for copy in near:
        copy.start()

    own_x.wait()
    remote(x_hbm, xpair.at[oc], d2d_s.at[0], d2d_r.at[0], partner).wait_recv()
    mine = slot(p, s)
    for d in (1, 3, 2, 0):
        ss = wrap(s + d)
        for pp in range(RING):
            feat = pl.multiple_of(
                jnp.where(first, DEPTH * ss + 256 * pp, DEPTH * pp + 256 * ss), 256
            )
            rows = jnp.concatenate(
                [xpair[0, :, pl.ds(feat, 256)].astype(F32), xpair[1, :, pl.ds(feat, 256)].astype(F32)],
                axis=0,
            ).astype(BF16)
            if d == 0:
                xall[mine, :, 256 * pp : 256 * pp + 256] = rows
            else:
                xs[d, :, 256 * pp : 256 * pp + 256] = rows
        if d:
            copy = remote(xs.at[d], xall.at[mine], x1_s.at[d], x_r.at[mine], device(p, ss))
            copy.start()
            sends.append(copy)

    far = [weights(other, 2) for other in (0, 1)]
    weights(1, 0).start()
    weights(0, 0)
    x_d2d.wait_send()
    wo_d2d = remote(
        wo_hbm.at[:, pl.ds(pl.multiple_of(oc * HALF, HALF), HALF)], wo2.at[c],
        d2d_s.at[1], d2d_r.at[1], partner,
    )
    wo_d2d.start()

    def arrived(m):
        remote(xall.at[m], xall.at[m], x1_s.at[0], x_r.at[m], partner).wait_recv()

    def from_plane(e):
        for other in (0, 1):
            k = 2 * wrap(p + e) + (oc if other else c)
            here = wall.at[k, moved]
            remote(here, here, w_s.at[0], w_r.at[k], partner).wait_recv()
            dz = -1 if other else 1
            copy = remote(here, here, z_s.at[k], z_r.at[k], t, dz)
            pl.when(beyond[dz])(copy.start)
            forwards.append((beyond[dz], copy))
            if e == 2:
                last = z == (planes - 2 if other else 1)
                copy = remote(here, here, e_s.at[RING * other + e], z_r.at[k], t, -dz)
                pl.when(last)(copy.start)
                forwards.append((last, copy))

    def forward(d):
        m = slot(p, wrap(s + d))
        if d:
            arrived(m)
        for e in (1, 3, 2):
            copy = remote(
                xall.at[m], xall.at[m], x2_s.at[RING * e + d], x_r.at[m], device(wrap(p + e), s)
            )
            copy.start()
            sends.append(copy)

    eye = lax.broadcasted_iota(jnp.int32, (HEAD, HEAD), 0) == lax.broadcasted_iota(
        jnp.int32, (HEAD, HEAD), 1
    )
    sign = jnp.where(lax.broadcasted_iota(jnp.int32, (HEAD, HEAD), 1) < HEAD // 2, -1.0, 1.0)

    def table(n, _):
        at = pl.ds(pl.multiple_of(n * HEAD, HEAD), HEAD)
        line = pos_ref[at].astype(F32)
        column = jnp.sum(jnp.where(eye, line[None, :], 0.0), axis=1, keepdims=True)
        ang = column * freq_ref[...]
        cos_t[at, :] = jnp.cos(ang)
        sin_t[at, :] = jnp.sin(ang) * sign
        return 0

    own_pos.wait()
    own_freq.wait()
    lax.fori_loop(0, SPAN // HEAD, table, 0)

    for copy in near:
        copy.wait_send()
        sends.remove(copy)
    for copy in far:
        copy.start()
    for alone, fill, copy in extra:

        @pl.when(alone)
        def _(fill=fill, copy=copy):
            fill(brought)
            copy.start()

    from_plane(1)
    from_plane(3)
    for d in range(RING):
        forward(d)
    from_plane(2)
    own_o.wait()
    wo_d2d.wait()
    k = 2 * p + oc
    remote(wall.at[k], wall.at[k], w_s.at[0], w_r.at[k], partner).wait_recv()
    for e in (1, 3, 2):
        for other in (0, 1):
            k = 2 * wrap(p + e) + (oc if other else c)
            there = wall.at[k, brought]
            remote(there, there, z_s.at[k], z_r.at[k], partner).wait_recv()
    for e in (1, 3, 2):
        for ss in range(RING):
            arrived(slot(wrap(p + e), ss))

    q_sends = []

    def partial(i):
        at = pl.ds(i * ROWS, ROWS)
        r = jnp.dot(
            xall[RING * i : RING * i + RING].reshape(ROWS, DEPTH),
            wall[...].reshape(DEPTH, KV_COLS + Q_COLS),
            preferred_element_type=F32,
        ).astype(BF16)
        for ss in range(RING):
            ykv[ss, at, :] = r[:, ss * HEAD : (ss + 1) * HEAD]
            yq[i, ss] = r[:, KV_COLS + ss * 2 * HEAD : KV_COLS + (ss + 1) * 2 * HEAD]

    def send_kv(i):
        at = pl.ds(i * ROWS, ROWS)
        for d in (2, 1, 3):
            ss = wrap(s + d)
            copy = remote(
                ykv.at[ss, at], ykv_in.at[s, at], ykv_s.at[i, d], ykv_r.at[i, s], device(p, ss)
            )
            copy.start()
            sends.append(copy)

    def send_q(i):
        group = []
        for d in (2, 1, 3):
            ss = wrap(s + d)
            copy = remote(yq.at[i, ss], yq_in.at[i, s], yq_s.at[i, d], yq_r.at[i, s], device(p, ss))
            copy.start()
            group.append(copy)
        q_sends.append(group)

    def sent_q(i):
        for copy in q_sends[i]:
            copy.wait_send()

    def gather_kv(i):
        at = pl.ds(i * ROWS, ROWS)
        total = ykv[s, at, :].astype(F32)
        for d in (1, 2, 3):
            ss = wrap(s + d)
            remote(
                ykv.at[ss, at], ykv_in.at[ss, at], ykv_s.at[i, d], ykv_r.at[i, ss], partner
            ).wait_recv()
            total += ykv_in[ss, at, :].astype(F32)
        whole = total.astype(BF16).astype(F32)
        turned = whole * cos_t[at, :] + pltpu.roll(whole, HEAD // 2, 1) * sin_t[at, :]
        kv[c, at, :] = jnp.where(first, turned, whole).astype(BF16)
        copy = remote(kv.at[c, at], kv.at[c, at], kv_s.at[i], kv_r.at[i], partner)
        copy.start()
        sends.append(copy)

    def attend(i):
        at = pl.ds(i * ROWS, ROWS)
        remote(kv.at[oc, at], kv.at[oc, at], kv_s.at[i], kv_r.at[i], partner).wait_recv()
        total = yq[i, s].astype(F32)
        for d in (1, 2, 3):
            ss = wrap(s + d)
            remote(yq.at[i, ss], yq_in.at[i, ss], yq_s.at[i, d], yq_r.at[i, ss], partner).wait_recv()
            total += yq_in[i, ss].astype(F32)
        keys = (i + 1) * ROWS
        row = i * ROWS + lax.broadcasted_iota(jnp.int32, (ROWS, keys), 0)
        seen = lax.broadcasted_iota(jnp.int32, (ROWS, keys), 1) <= row
        for h in range(2):
            v = total[:, h * HEAD : (h + 1) * HEAD]
            q = (v * cos_t[at, :] + pltpu.roll(v, HEAD // 2, 1) * sin_t[at, :]).astype(BF16)
            scores = lax.dot_general(
                q, kv[0, :keys, :], (((1,), (1,)), ((), ())), preferred_element_type=F32
            )
            scores = jnp.where(seen, scores, -jnp.inf)
            top = jnp.max(scores, axis=1, keepdims=True)
            expo = jnp.exp2((scores - top) * EXP_SCALE)
            norm = jnp.sum(expo, axis=1, keepdims=True)
            head = jnp.dot(expo.astype(BF16), kv[1, :keys, :], preferred_element_type=F32) / norm
            hbuf[c, i, :, h * HEAD : (h + 1) * HEAD] = head.astype(BF16)
        copy = remote(hbuf.at[c, i], hbuf.at[c, i], h_s.at[i], h_r.at[i], partner)
        copy.start()
        sends.append(copy)

    def project(i):
        remote(hbuf.at[oc, i], hbuf.at[oc, i], h_s.at[i], h_r.at[i], partner).wait_recv()
        far_place = wrap(p + 2)
        for w in range(2):
            cols = pl.ds(w * WIDE, WIDE)
            r = jnp.dot(hbuf[0, i], wo2[0, :, cols], preferred_element_type=F32)
            r += jnp.dot(hbuf[1, i], wo2[1, :, cols], preferred_element_type=F32)
            r = r.astype(BF16)
            for b in range(RING):
                for v in range(2):
                    g = 2 * w + v
                    obuf[i, jnp.where(first, b, g), jnp.where(first, g, b)] = r[
                        b * TOK : (b + 1) * TOK, v * PART : (v + 1) * PART
                    ]
        if i == RING - 1:
            for d, w in ((2, 2), (1, 0), (3, 1)):
                place = wrap(p + d)
                copy = remote(
                    obuf.at[i, place], o1_in.at[i, w], o1_s.at[i, w], o1_r.at[i, w], device(place, s)
                )
                copy.start()
                sends.append(copy)
            return
        for d, w in ((1, 0), (3, 1)):
            copy = remote(
                obuf.at[i, far_place, pl.ds(2 * w, 2)], f_in.at[i, w], f_s.at[i, w], f_r.at[i, w],
                device(wrap(p + d), s),
            )
            copy.start()
            sends.append(copy)

    def fold(i):
        for d, w in ((1, 0), (3, 1)):
            place, half = wrap(p + d), pl.ds(2 * w, 2)
            remote(f_in.at[i, w], f_in.at[i, w], f_s.at[i, w], f_r.at[i, w], partner).wait_recv()
            obuf[i, place, half] = (
                obuf[i, place, half].astype(F32) + f_in[i, w].astype(F32)
            ).astype(BF16)
            copy = remote(
                obuf.at[i, place], o1_in.at[i, w], o1_s.at[i, w], o1_r.at[i, w], device(place, s)
            )
            copy.start()
            sends.append(copy)

    def combine(i):
        total = obuf[i, p].astype(F32)
        for w in range(3 if i == RING - 1 else 2):
            remote(o1_in.at[i, w], o1_in.at[i, w], o1_s.at[i, w], o1_r.at[i, w], partner).wait_recv()
            total += o1_in[i, w].astype(F32)
        o1_sum[i] = total.astype(BF16)
        for d in (2, 1, 3):
            ss = wrap(s + d)
            copy = remote(
                o1_sum.at[i, ss], o2_in.at[i, s], o2_s.at[i, d], o2_r.at[i, s], device(p, ss)
            )
            copy.start()
            sends.append(copy)

    def final(i, core):
        return remote(
            fin_out.at[i, core], fin_in.at[c, y], fin_s.at[i, core], fin_r.at[c, y],
            8 * i + 2 * x + core,
        )

    def finish(i):
        total = o1_sum[i, s].astype(F32)
        for d in (1, 2, 3):
            ss = wrap(s + d)
            remote(o1_sum.at[i, 0], o2_in.at[i, ss], o2_s.at[i, d], o2_r.at[i, ss], partner).wait_recv()
            total += o2_in[i, ss].astype(F32)
        for core in range(2):
            rows = total[core * (TOK // 2) : (core + 1) * (TOK // 2)].astype(BF16)
            fin_out[i, core] = rows
            mine_now = jnp.logical_and(y == i, c == core)

            @pl.when(mine_now)
            def _(rows=rows):
                fin_in[c, y] = rows

            @pl.when(jnp.logical_not(mine_now))
            def _(core=core):
                final(i, core).start()

    partial(0)
    send_kv(0)
    send_q(0)
    partial(1)
    partial(2)
    partial(3)
    send_kv(1)
    send_q(1)
    send_kv(2)
    send_kv(3)
    gather_kv(0)
    sent_q(0)
    send_q(2)
    gather_kv(1)
    sent_q(1)
    send_q(3)
    attend(0)
    attend(1)
    project(0)
    gather_kv(2)
    project(1)
    gather_kv(3)
    fold(0)
    attend(2)
    fold(1)
    attend(3)
    project(2)
    combine(0)
    project(3)
    fold(2)
    combine(1)
    finish(0)
    combine(2)
    finish(1)
    combine(3)
    finish(2)
    finish(3)

    sent_q(2)
    sent_q(3)
    for copy in sends:
        copy.wait_send()
    for alone, _, copy in extra:
        pl.when(alone)(copy.wait_send)
    for active, copy in forwards:
        pl.when(active)(copy.wait_send)
    for i in range(RING):
        for core in range(2):

            @pl.when(jnp.logical_or(y != i, c != core))
            def _(i=i, core=core):
                final(i, core).wait_send()

    for cc in range(2):
        for yy in range(RING):

            @pl.when(jnp.logical_or(y != yy, c != cc))
            def _(cc=cc, yy=yy):
                remote(
                    fin_out.at[0, 0], fin_in.at[cc, yy], fin_s.at[0, 0], fin_r.at[cc, yy], partner
                ).wait_recv()

            col = cc * HALF + yy * PART
            out_ref[:, col : col + PART] = fin_in[cc, yy]


def shards(hidden_in, query_weight, key_weight, value_projection_weight, output_weight, head_order, positions):
    half = np.float32(ROPE_BASE) ** (
        np.float32(-2.0) * np.arange(HEAD // 2, dtype=np.float32) / np.float32(HEAD)
    )
    freq = jnp.asarray(np.concatenate([half, half])[None, :])
    vmem, dma = pltpu.VMEM, pltpu.SemaphoreType.DMA
    any_spec = pl.BlockSpec(memory_space=pl.ANY)
    vmem_spec = pl.BlockSpec(memory_space=vmem)
    return pl.pallas_call(
        kernel,
        out_shape=pltpu.VMEM((TOK // 2, FEAT), BF16),
        in_specs=[any_spec] * 5 + [pl.BlockSpec(memory_space=pltpu.SMEM), any_spec, any_spec],
        out_specs=vmem_spec,
        scratch_shapes=[
            vmem((2, TOK // 2, FEAT), BF16),
            vmem((RING, TOK, DEPTH), BF16),
            vmem((RING * RING, TOK, DEPTH), BF16),
            vmem((HEADS, W_ROWS, HEAD), BF16),
            vmem((2, W_ROWS, 1024), BF16),
            vmem((2 * RING, W_ROWS, KV_COLS + Q_COLS), BF16),
            vmem((2 * RING, W_ROWS, KV_COLS + Q_COLS), BF16),
            vmem((2, 2 * HEAD, HALF), BF16),
            vmem((8, HEAD), jnp.int32),
            pltpu.SMEM((8, HEAD), jnp.int32),
            vmem((SPAN, HEAD), F32),
            vmem((SPAN, HEAD), F32),
            vmem((RING, SPAN, HEAD), BF16),
            vmem((RING, SPAN, HEAD), BF16),
            vmem((RING, RING, ROWS, 2 * HEAD), BF16),
            vmem((RING, RING, ROWS, 2 * HEAD), BF16),
            vmem((2, SPAN, HEAD), BF16),
            vmem((2, RING, ROWS, 2 * HEAD), BF16),
            vmem((RING, RING, RING, TOK, PART), BF16),
            vmem((RING, 2, 2, TOK, PART), BF16),
            vmem((RING, 3, RING, TOK, PART), BF16),
            vmem((RING, RING, TOK, PART), BF16),
            vmem((RING, RING, TOK, PART), BF16),
            vmem((RING, 2, TOK // 2, PART), BF16),
            vmem((2, RING, TOK // 2, PART), BF16),
            vmem((SPAN,), jnp.int32),
            vmem((1, HEAD), F32),
            dma((8,)), dma((2,)), dma((2,)),
            dma((2 * RING,)), dma((2 * RING,)), dma((2 * RING,)), dma((2 * RING,)), dma((2 * RING,)),
            dma((RING,)), dma((RING * RING,)), dma((RING * RING,)),
            dma((RING, RING)), dma((RING, RING)), dma((RING, RING)), dma((RING, RING)),
            dma((RING,)), dma((RING,)), dma((RING,)), dma((RING,)),
            dma((RING, 2)), dma((RING, 2)), dma((RING, 3)), dma((RING, 3)),
            dma((RING, RING)), dma((RING, RING)), dma((RING, 2)), dma((2, RING)),
        ],
        compiler_params=pltpu.CompilerParams(
            collective_id=0, has_side_effects=True, vmem_limit_bytes=56 << 20
        ),
        cost_estimate=pl.CostEstimate(flops=6 << 30, bytes_accessed=8 << 20, transcendentals=1 << 20),
    )(hidden_in, query_weight, key_weight, value_projection_weight, output_weight, head_order, positions, freq)


def solution(mesh):
    return jax.shard_map(
        shards,
        mesh=mesh,
        in_specs=(
            P(("replica", "tensor"), None),
            P("tensor", None),
            P("tensor", None),
            P("tensor", None),
            P("tensor", None),
            P(),
            P("replica"),
        ),
        out_specs=P(("replica", "tensor"), None),
        check_vma=False,
    )
```
